128 devices in a mesh: dp: 4 (over y), lists: 32 (over z, x, core).
Axes of the slice: x: 4, y: 4, z: 4, core: 2. Of those that a mesh axis runs over, the one named last changes fastest.
Arguments:
- embeddings: bfloat16 [131072, 1024], P('dp', 'lists'), may hold values from -6 to 6
- assign: int32 [131072], P(('dp', 'lists')), may hold values from 0 to 65535, as said below
- list_slot: int32 [65536], replicated, may hold values from 0 to 65535, as said below
- centroids: bfloat16 [65536, 1024], P('lists'), may hold values from -3 to 3
- rotation: bfloat16 [32, 1024, 1024], P('lists'), may hold values from -0.1875 to 0.1875
- codebook: bfloat16 [16, 256, 64], replicated, may hold values from -6 to 6
Outputs:
- quant_error: float32 [16, 131072], P(None, ('dp', 'lists'))
The draws below stay inside these ranges and needn't reach their ends.
Inputs may be any that keep to these rules, and one draw needn't show every extreme that they name: A permutation of the lists; list l belongs to the group list_slot[l] // 2048. `assign`: among the 1024 vectors of one device (aligned blocks in order), at most 96 belong to the lists of any one group, and one group, the same for every device, gets exactly 96 from each device.
All inputs are finite; a program needn't handle non-finite values.
Results may differ from the reference program's by a relative error of at most 0.0016.
Values may be sent and summed in bfloat16 or wider, within the bound.
A program may use at most 128 MiB of HBM per device.

```python
import jax
import jax.numpy as jnp
from jax import lax

D = 1024
M = 16
K = 256
DS = 64
LISTS_DEV = 2048
ROWS_DEV = 1024
LISTS = 65536
GROUPS = 32
CAP = 96
VECS = 131072
N_LISTS = 32


def routing_tables(key):
    permuted = jax.random.permutation(jax.random.fold_in(key, 7), LISTS).astype(jnp.int32)
    inverse = jnp.argsort(permuted, stable=True).astype(jnp.int32)
    return (permuted, inverse)


def draw_list_slot(key, part):
    permuted, inverse = routing_tables(key)
    return permuted


def draw_assign(key, part):
    permuted, inverse = routing_tables(key)
    block_count = VECS // ROWS_DEV
    spare_rows = ROWS_DEV - CAP
    hot_owner = jax.random.randint(jax.random.fold_in(key, 8), (), 0, N_LISTS).astype(jnp.int32)
    offsets = jax.random.randint(jax.random.fold_in(key, 9), (block_count, spare_rows), 0, 2).astype(jnp.int32)
    cyclic = (jnp.arange(spare_rows, dtype=jnp.int32)[None, :] + offsets) % (N_LISTS - 1)
    others = (hot_owner + 1 + cyclic) % N_LISTS
    hot_rows = jnp.full((block_count, CAP), hot_owner, jnp.int32)
    owner_rows = jnp.concatenate([hot_rows, others.astype(jnp.int32)], axis=1)
    block_keys = jax.random.split(jax.random.fold_in(key, 10), block_count)
    shuffled = jax.vmap(lambda one_key, row_owner: jax.random.permutation(one_key, row_owner))(block_keys, owner_rows)
    within_list = jax.random.randint(jax.random.fold_in(key, 11), (block_count, ROWS_DEV), 0, LISTS_DEV).astype(jnp.int32)
    slot_index = shuffled.astype(jnp.int32) * LISTS_DEV + within_list
    return jnp.take(inverse, slot_index.reshape(-1)).astype(jnp.int32)


def levels(own_key, dims, pieces, low, largest):
    level, own = 1.0, jax.random.fold_in(own_key, 6)
    for dim, shards_of in pieces:
        draws = jnp.exp(jax.random.uniform(jax.random.fold_in(own, dim), (shards_of,), jnp.float32, low / len(pieces), largest / len(pieces)))
        level = level * jnp.repeat(draws, dims[dim] // shards_of).reshape([-1 if axis == dim else 1 for axis in range(len(dims))])
    return level


def normal_values(key, dims, width, bound, shards=(), held_as=jnp.bfloat16):
    loudness = levels(key, dims, shards, -0.22, 0.18) if shards else 1.0
    result = jax.random.normal(key, dims, jnp.float32) * width * loudness
    return jnp.minimum(jnp.maximum(result, -bound), bound).astype(held_as)


def setup_inputs(seed: int = 0) -> dict:
    seeds = jax.random.split(jax.random.key(seed), 7)
    embeddings = normal_values(seeds[0], (VECS, D), 1.0, 6.0, ((0, 4), (1, 32)))
    assign = draw_assign(jax.random.fold_in(seeds[6], 71), 0)
    list_slot = draw_list_slot(jax.random.fold_in(seeds[6], 71), 0)
    centroids = normal_values(seeds[3], (LISTS, D), 0.5, 3.0, ((0, 32),))
    rotation = normal_values(seeds[4], (GROUPS, D, D), D ** -0.5, 0.1875, ((0, 32),))
    codebook = normal_values(seeds[5], (M, K, DS), 1.0, 6.0)
    return dict(embeddings=embeddings, assign=assign, list_slot=list_slot, centroids=centroids, rotation=rotation, codebook=codebook)


def reference(embeddings, assign, list_slot, centroids, rotation, codebook):
    slot_index = jnp.take(list_slot, assign).astype(jnp.int32)
    group_of = (slot_index // LISTS_DEV).astype(jnp.int32)
    centre_rows = jnp.take(centroids, slot_index, axis=0)
    residual = (embeddings.astype(jnp.float32) - centre_rows.astype(jnp.float32)).astype(jnp.bfloat16)
    sorted_order = jnp.argsort(group_of, stable=True).astype(jnp.int32)
    block_count = VECS // ROWS_DEV
    sorted_rows = jnp.take(residual, sorted_order, axis=0).reshape(block_count, ROWS_DEV, D)
    sorted_groups = jnp.take(group_of, sorted_order).reshape(block_count, ROWS_DEV)

    def rotate_block(pair):
        block_rows, block_groups = pair
        wide_rows = block_rows.astype(jnp.float32)

        def apply_group(group_index, total):
            matrix = lax.dynamic_index_in_dim(rotation, group_index, 0, keepdims=False).astype(jnp.float32)
            image = jnp.dot(wide_rows, matrix, precision=lax.Precision.HIGHEST, preferred_element_type=jnp.float32)
            return jnp.where((block_groups == group_index)[:, None], image, total)

        start = jnp.zeros((ROWS_DEV, D), jnp.float32)
        first_group = block_groups[0].astype(jnp.int32)
        last_group = (block_groups[ROWS_DEV - 1] + 1).astype(jnp.int32)
        return lax.fori_loop(first_group, last_group, apply_group, start).astype(jnp.bfloat16)

    rotated_sorted = lax.map(rotate_block, (sorted_rows, sorted_groups)).reshape(VECS, D)
    rotated = jnp.zeros((VECS, D), jnp.bfloat16).at[sorted_order].set(rotated_sorted)
    code_norms = jnp.sum(jnp.square(codebook.astype(jnp.float32)), axis=2)

    def one_book(book_index):
        subspace = lax.dynamic_slice_in_dim(rotated, book_index * DS, DS, 1)
        codewords = lax.dynamic_index_in_dim(codebook, book_index, 0, keepdims=False)
        norm_row = lax.dynamic_index_in_dim(code_norms, book_index, 0, keepdims=False)
        products = lax.dot_general(subspace, codewords, (((1,), (1,)), ((), ())), preferred_element_type=jnp.float32)
        lengths = jnp.sum(jnp.square(subspace.astype(jnp.float32)), axis=1)
        distance = lengths[:, None] + norm_row[None, :] - 2.0 * products
        return jnp.min(distance, axis=1) / DS

    return lax.map(one_book, jnp.arange(M, dtype=jnp.int32))
```

```python
import functools

import jax
import jax.numpy as jnp
from jax import lax
from jax.experimental import pallas as pl
from jax.experimental.pallas import tpu as pltpu
from jax.sharding import PartitionSpec as P

MESH = pl.DeviceIdType.MESH
F32 = jnp.float32
BF16 = jnp.bfloat16
I32 = jnp.int32

N = 32
CAP = 96
HOME = 1024
D = 1024
FS = 32
LISTS = 2048
BOOKS, CODES, SUB = 16, 256, 64
CHUNKS = 4
CH = N * CAP // CHUNKS
QUAD = 4 * CAP


def dot(a, b):
    return jnp.dot(a, b, preferred_element_type=F32)


def iota(shape, dim):
    return lax.broadcasted_iota(I32, shape, dim)


def routes(assign_ref, slots_ref):
    assigned = assign_ref[...]
    table = slots_ref[...].astype(F32).T.astype(I32)
    table = jnp.concatenate([table >> 8, table & 255], axis=0).astype(F32).astype(BF16)
    rows = (iota((512, HOME), 0) == (assigned >> 7)).astype(F32).astype(BF16)
    picked = dot(table, rows)
    low = iota((128, HOME), 0) == (assigned & 127)
    upper = jnp.sum(jnp.where(low, picked[:128], 0.0), axis=0, keepdims=True)
    lower = jnp.sum(jnp.where(low, picked[128:], 0.0), axis=0, keepdims=True)
    slot = upper.astype(I32) * 256 + lower.astype(I32)
    target, local = slot >> 11, slot & (LISTS - 1)
    mine = iota((N, HOME), 0) == target
    onehot = mine.astype(F32)
    before = (iota((HOME, HOME), 0) < iota((HOME, HOME), 1)).astype(F32).astype(BF16)
    ahead = dot(onehot.astype(BF16), before)
    position = jnp.sum(jnp.where(mine, ahead, 0.0), axis=0, keepdims=True).astype(I32)
    place = (iota((128, HOME), 0) == position).astype(F32).astype(BF16)
    vector = iota((1, HOME), 1)
    fields = [vector & 255, vector >> 8, local & 255, local >> 8]
    planes = [jnp.where(mine, field.astype(F32), 0.0) for field in fields] + [onehot]
    planes = jnp.concatenate(planes, axis=0).astype(BF16)
    held = lax.dot_general(planes, place, (((1,), (1,)), ((), ())), preferred_element_type=F32).astype(I32)
    index, group, local_low, local_high, valid = (held[N * j : N * (j + 1)] for j in range(5))
    group = jnp.where(valid > 0, group, 32)
    entry = index + (group << 8) + (local_low << 14) + (local_high << 22)
    return target * 128 + position, entry


def kernel(
    emb_ref, assign_ref, slots_ref, cent_ref, rot_ref, book_ref, out_ref,
    xb, send, recv, near, cent, cent_t, rot, rot_t, codes, tab_own, tab_all, tab, resid, sub, errs,
    code_ref, ret_send, ret_recv,
    x_sem, c_sem, r_sem, tab_ss, tab_rs, vec_ss, vec_rs, ret_ss, ret_rs,
):
    me = lax.axis_index("lists")

    def peer(k):
        return lax.rem(me + k, N)

    barrier = pltpu.get_barrier_semaphore()

    @pl.loop(1, N)
    def _(k):
        pl.semaphore_signal(barrier, inc=1, device_id={"lists": peer(k)}, device_id_type=MESH)

    def x_copy(t):
        block = t // 8
        group = t - block * 8
        return pltpu.make_async_copy(
            emb_ref.at[:, pl.ds(pl.multiple_of(t * 256, 256), 256)],
            xb.at[block, pl.ds(pl.multiple_of(group * FS, FS), FS), :],
            x_sem.at[t],
        )

    @pl.loop(0, 128)
    def _(t):
        x_copy(t).start()

    c_copy = pltpu.make_async_copy(cent_ref, cent, c_sem)
    r_copy = pltpu.make_async_copy(rot_ref, rot, r_sem)
    c_copy.start()
    r_copy.start()

    code, entry = routes(assign_ref, slots_ref)
    code_ref[...] = code
    tab_own[...] = entry

    pl.semaphore_wait(barrier, N - 1)

    def tab_copy(k, home):
        return pltpu.make_async_remote_copy(
            src_ref=tab_own,
            dst_ref=tab_all.at[home],
            send_sem=tab_ss.at[k],
            recv_sem=tab_rs.at[k],
            device_id={"lists": peer(k)},
            device_id_type=MESH,
        )

    @pl.loop(1, N)
    def _(k):
        tab_copy(k, me).start()

    tab_all[me] = entry

    @pl.loop(0, 128)
    def _(t):
        x_copy(t).wait()

    @pl.loop(1, N)
    def _(k):
        tab_copy(k, lax.rem(me + N - k, N)).wait_recv()

    lane = iota((N, 128), 1)

    @pl.loop(0, N // 4)
    def _(q):
        parts = [tab_all[4 * q + j] + (j << 10) for j in range(4)]
        rolled = [parts[0]] + [pltpu.roll(parts[j], 128 - 32 * j, 1) for j in range(1, 4)]
        base = pl.multiple_of(q * QUAD, 128)
        for j in range(3):
            tab[:, pl.ds(base + 128 * j, 128)] = jnp.where(lane < 96 - 32 * j, rolled[j], rolled[j + 1])

    def select(owner, q):
        entries = tab[pl.ds(owner, 1), pl.ds(pl.multiple_of(q * QUAD, 128), QUAD)]
        index, group = entries & 255, (entries >> 8) & 63
        onehot = (iota((256, QUAD), 0) == index).astype(F32).astype(BF16)
        halves = []
        for half in range(2):
            lanes = slice(128 * half, 128 * half + 256)
            every = dot(xb[2 * q + half], onehot[:, lanes])
            groups = jnp.broadcast_to(group[:, lanes], (FS, 256))
            kept = jnp.zeros((FS, 256), F32)
            for g in range(8):
                kept = jnp.where(groups == g + 8 * half, every[FS * g : FS * (g + 1)], kept)
            halves.append(kept)
        left, right = halves
        return jnp.concatenate([left[:, :128], left[:, 128:] + right[:, :128], right[:, 128:]], axis=1).astype(BF16)

    def vec_copy(c, k, slice_of):
        return pltpu.make_async_remote_copy(
            src_ref=send.at[c, k],
            dst_ref=recv.at[c, pl.ds(pl.multiple_of(slice_of * FS, FS), FS), :],
            send_sem=vec_ss.at[c, k],
            recv_sem=vec_rs.at[c, k],
            device_id={"lists": peer(k)},
            device_id_type=MESH,
        )

    @pl.loop(0, CHUNKS)
    def _(c):
        @pl.loop(1, N)
        def _(k):
            for j in range(2):
                send[c, k, :, QUAD * j : QUAD * (j + 1)] = select(peer(k), 2 * c + j)
            vec_copy(c, k, me).start()

        for j in range(2):
            recv[c, pl.ds(pl.multiple_of(me * FS, FS), FS), QUAD * j : QUAD * (j + 1)] = select(me, 2 * c + j)

    c_copy.wait()
    r_copy.wait()

    @pl.loop(0, 4)
    def _(i):
        @pl.loop(0, 4)
        def _(j):
            rows, columns = pl.multiple_of(i * 256, 256), pl.multiple_of(j * 256, 256)
            rot_t[pl.ds(columns, 256), pl.ds(rows, 256)] = rot[pl.ds(rows, 256), pl.ds(columns, 256)].T

    @pl.loop(0, 8)
    def _(i):
        @pl.loop(0, 4)
        def _(j):
            rows, columns = pl.multiple_of(i * 256, 256), pl.multiple_of(j * 256, 256)
            cent_t[pl.ds(columns, 256), pl.ds(rows, 256)] = cent[pl.ds(rows, 256), pl.ds(columns, 256)].T

    @pl.loop(0, BOOKS)
    def _(m):
        words = book_ref[m].astype(F32)
        norm = jnp.sum(words * words, axis=0, keepdims=True)
        first = norm.astype(BF16).astype(F32)
        second = (norm - first).astype(BF16).astype(F32)
        third = norm - first - second
        row = iota((SUB, CODES), 0)
        extra = jnp.where(row == 0, first, jnp.where(row == 1, second, jnp.where(row == 2, third, 0.0)))
        codes[m] = jnp.concatenate([words * -2.0, extra], axis=0).T.astype(BF16)

    sub[:, SUB:, :] = jnp.ones((4, SUB, CH), BF16)

    @pl.loop(0, N * CAP // 256)
    def _(t):
        lanes = pl.ds(pl.multiple_of(t * 256, 256), 256)
        local = tab[pl.ds(me, 1), lanes] >> 14
        onehot = (iota((LISTS, 256), 0) == local).astype(F32).astype(BF16)

        @pl.loop(0, 4)
        def _(i):
            rows = pl.ds(pl.multiple_of(i * 256, 256), 256)
            near[rows, lanes] = dot(cent_t[rows, :], onehot).astype(BF16)

    def ret_copy(home, owner):
        return pltpu.make_async_remote_copy(
            src_ref=ret_send.at[home],
            dst_ref=ret_recv.at[owner],
            send_sem=ret_ss.at[home],
            recv_sem=ret_rs.at[owner],
            device_id={"lists": home},
            device_id_type=MESH,
        )

    wide = iota((BOOKS, 128), 1)

    @pl.loop(0, CHUNKS)
    def _(c):
        @pl.loop(1, N)
        def _(k):
            vec_copy(c, k, lax.rem(me + N - k, N)).wait_recv()

        lanes = pl.ds(pl.multiple_of(c * CH, 256), CH)

        @pl.loop(0, 4)
        def _(i):
            rows = pl.ds(pl.multiple_of(i * 256, 256), 256)
            resid[rows, :] = (recv[c, rows, :].astype(F32) - near[rows, lanes].astype(F32)).astype(BF16)

        @pl.loop(0, 4)
        def _(i):
            rows = pl.ds(pl.multiple_of(i * 256, 256), 256)
            turned = dot(rot_t[rows, :], resid[...]).astype(BF16)
            for j in range(4):
                piece = turned[SUB * j : SUB * (j + 1)]
                sub[j, :SUB, :] = piece
                squares = piece.astype(F32)
                length = jnp.sum(squares * squares, axis=0, keepdims=True)
                least = jnp.min(dot(codes[4 * i + j], sub[j]), axis=0, keepdims=True)
                errs[pl.ds(4 * i + j, 1), :] = (length + least) * (1.0 / SUB)

        for q in range(2):
            tiles = [errs[:, QUAD * q + 128 * j : QUAD * q + 128 * (j + 1)] for j in range(3)]
            pieces = [
                tiles[0],
                pltpu.roll(jnp.where(wide < 64, tiles[1], tiles[0]), 32, 1),
                pltpu.roll(jnp.where(wide < 32, tiles[2], tiles[1]), 64, 1),
                pltpu.roll(tiles[2], 96, 1),
            ]
            for j in range(4):
                home = 8 * c + 4 * q + j
                piece = jnp.where(wide < CAP, pieces[j], 0.0)
                ret_send[home] = piece

                @pl.when(home == me)
                def _():
                    ret_recv[home] = piece

                @pl.when(home != me)
                def _():
                    ret_copy(home, me).start()

    @pl.loop(1, N)
    def _(k):
        ret_copy(me, peer(k)).wait_recv()

    def spread(t, total):
        got = jnp.concatenate([ret_recv[2 * t], ret_recv[2 * t + 1]], axis=1)
        high = got.astype(BF16)
        low = (got - high.astype(F32)).astype(BF16)
        onehot = (iota((256, HOME), 0) + 256 * t == code_ref[...]).astype(F32).astype(BF16)
        return total + dot(jnp.concatenate([high, low], axis=0), onehot)

    total = lax.fori_loop(0, N // 2, spread, jnp.zeros((2 * BOOKS, HOME), F32))
    out_ref[...] = total[:BOOKS] + total[BOOKS:]

    @pl.loop(1, N)
    def _(k):
        tab_copy(k, me).wait_send()
        ret_copy(peer(k), me).wait_send()

        @pl.loop(0, CHUNKS)
        def _(c):
            vec_copy(c, k, me).wait_send()


def shards(embeddings, assign, list_slot, centroids, rotation, codebook):
    vmem = pl.BlockSpec(memory_space=pltpu.VMEM)
    hbm = pl.BlockSpec(memory_space=pl.ANY)
    dma = pltpu.SemaphoreType.DMA
    return pl.pallas_call(
        kernel,
        out_shape=jax.ShapeDtypeStruct((BOOKS, HOME), F32),
        in_specs=[hbm, vmem, vmem, hbm, hbm, vmem],
        out_specs=vmem,
        scratch_shapes=[
            pltpu.VMEM((16, 256, 256), BF16),
            pltpu.VMEM((CHUNKS, N, FS, CH), BF16),
            pltpu.VMEM((CHUNKS, D, CH), BF16),
            pltpu.VMEM((D, N * CAP), BF16),
            pltpu.VMEM((LISTS, D), BF16),
            pltpu.VMEM((D, LISTS), BF16),
            pltpu.VMEM((D, D), BF16),
            pltpu.VMEM((D, D), BF16),
            pltpu.VMEM((BOOKS, CODES, 2 * SUB), BF16),
            pltpu.VMEM((N, 128), I32),
            pltpu.VMEM((N, N, 128), I32),
            pltpu.VMEM((N, N * CAP), I32),
            pltpu.VMEM((D, CH), BF16),
            pltpu.VMEM((4, 2 * SUB, CH), BF16),
            pltpu.VMEM((BOOKS, CH), F32),
            pltpu.VMEM((1, HOME), I32),
            pltpu.VMEM((N, BOOKS, 128), F32),
            pltpu.VMEM((N, BOOKS, 128), F32),
            dma((128,)), dma, dma,
            dma((N,)), dma((N,)),
            dma((CHUNKS, N)), dma((CHUNKS, N)),
            dma((N,)), dma((N,)),
        ],
        compiler_params=pltpu.CompilerParams(
            collective_id=0, has_side_effects=True, vmem_limit_bytes=58 * 2**20
        ),
        name="encode",
    )(
        embeddings.T,
        assign.reshape(1, HOME),
        list_slot.reshape(512, 128),
        centroids,
        rotation.reshape(D, D),
        codebook.transpose(0, 2, 1),
    )


def solution(mesh):
    placed = (
        P("dp", "lists"),
        P(("dp", "lists")),
        P(),
        P("lists", None),
        P("lists", None, None),
        P(),
    )
    return jax.shard_map(
        shards, mesh=mesh, in_specs=placed, out_specs=P(None, ("dp", "lists")), check_vma=False
    )
```

```python
import jax
import jax.numpy as jnp
from jax import lax
from jax.experimental import pallas as pl
from jax.experimental.pallas import tpu as pltpu
from jax.sharding import PartitionSpec as P

MESH = pl.DeviceIdType.MESH
F32 = jnp.float32
BF16 = jnp.bfloat16
I32 = jnp.int32

N = 32
DP = 4
HOME = 1024
D = 1024
FS = 32
LISTS = 2048
BOOKS, CODES, SUB = 16, 256, 64
CAP = 42
OVER = 64
BLOCKS = 11
PARTS = ((0, 6), (6, 11))
FIRST = N * OVER
SLOTS = FIRST + 128 * BLOCKS
NEAR = 384
NOBODY = 32 << 8


def dot(a, b):
    return jnp.dot(a, b, preferred_element_type=F32)


def iota(shape, dim):
    return lax.broadcasted_iota(I32, shape, dim)


def onehots(mask):
    return mask.astype(F32).astype(BF16)


def routes(assign_ref, slots_ref):
    assigned = assign_ref[...]
    table = slots_ref[...].astype(F32).T.astype(I32)
    table = jnp.concatenate([table >> 8, table & 255], axis=0).astype(F32).astype(BF16)
    picked = dot(table, onehots(iota((512, HOME), 0) == (assigned >> 7)))
    low = iota((128, HOME), 0) == (assigned & 127)
    upper = jnp.sum(jnp.where(low, picked[:128], 0.0), axis=0, keepdims=True)
    lower = jnp.sum(jnp.where(low, picked[128:], 0.0), axis=0, keepdims=True)
    slot = upper.astype(I32) * 256 + lower.astype(I32)
    target, local = slot >> 11, slot & (LISTS - 1)
    mine = iota((N, HOME), 0) == target
    before = onehots(iota((HOME, HOME), 0) < iota((HOME, HOME), 1))
    ahead = dot(onehots(mine), before)
    rank = jnp.sum(jnp.where(mine, ahead, 0.0), axis=0, keepdims=True).astype(I32)
    over = rank >= CAP
    over_rank = dot(jnp.broadcast_to(onehots(over), (8, HOME)), before)[:1].astype(I32)
    segment = (target >= 11).astype(I32) + (target >= 22).astype(I32)
    row = jnp.where(over, 11, target - 11 * segment)
    lane = jnp.where(over, over_rank, CAP * segment + rank)
    mine = iota((16, HOME), 0) == row
    place = onehots(iota((128, HOME), 0) == lane)
    vector = iota((1, HOME), 1)
    fields = [vector & 255, vector >> 8, local & 255, local >> 8, jnp.ones_like(vector)]
    planes = [jnp.where(mine, field.astype(F32), 0.0) for field in fields]
    planes = jnp.concatenate(planes, axis=0).astype(BF16)
    held = lax.dot_general(planes, place, (((1,), (1,)), ((), ())), preferred_element_type=F32).astype(I32)
    index, group, local_low, local_high, valid = (held[16 * j : 16 * (j + 1)] for j in range(5))
    entry = index + (group << 8) + (local_low << 14) + (local_high << 22)
    entry = jnp.where(valid > 0, entry, NOBODY)
    return target * 128 + jnp.where(over, 64 + over_rank, rank), entry


def kernel(
    emb_ref, assign_ref, slots_ref, cent_ref, rot_ref, book_ref, out_ref, flag_ref,
    xb, send, recv, wide, near, cent, cent_t, rot, rot_t, codes, tab_own, tab_all, tab, tab_over, local_ref,
    resid, sub, errs, code_ref, ret_send, ret_recv, flag_own, flag_all,
    x_sem, c_sem, r_sem, own_sem, tab_ss, tab_rs, vec_ss, vec_rs, ret_ss, ret_rs, ag_ss, ag_rs, flag_ss, flag_rs,
):
    me = lax.axis_index("lists")
    replica = lax.axis_index("dp")
    core = lax.rem(me, 2)
    x = lax.rem(lax.div(me, 2), 4)
    z = lax.div(me, 8)

    def peer(k):
        return lax.rem(me + k, N)

    def back(k):
        return lax.rem(me + N - k, N)

    barrier = pltpu.get_barrier_semaphore()

    @pl.loop(1, N)
    def _(k):
        pl.semaphore_signal(barrier, inc=1, device_id={"lists": peer(k)}, device_id_type=MESH)

    for j in range(1, DP):
        other = lax.rem(replica + j, DP)
        pl.semaphore_signal(barrier, inc=1, device_id={"dp": other}, device_id_type=MESH)

    def x_copy(t):
        block = lax.div(t, 12)
        group = t - block * 12
        return pltpu.make_async_copy(
            emb_ref.at[:, pl.ds(pl.multiple_of(t * 256, 256), 256)],
            xb.at[block, pl.ds(pl.multiple_of(group * FS, FS), FS), :],
            x_sem.at[t],
        )

    @pl.loop(0, 128)
    def _(t):
        x_copy(t).start()

    c_copy = pltpu.make_async_copy(cent_ref, cent, c_sem)
    r_copy = pltpu.make_async_copy(rot_ref, rot, r_sem)
    c_copy.start()
    r_copy.start()

    code, entry = routes(assign_ref, slots_ref)
    code_ref[...] = code
    tab_own[...] = entry

    pl.semaphore_wait(barrier, N - 1 + DP - 1)

    def tab_copy(k, home):
        return pltpu.make_async_remote_copy(
            src_ref=tab_own,
            dst_ref=tab_all.at[home],
            send_sem=tab_ss.at[k],
            recv_sem=tab_rs.at[k],
            device_id={"lists": peer(k)},
            device_id_type=MESH,
        )

    @pl.loop(1, N)
    def _(k):
        tab_copy(k, me).start()

    tab_all[me] = entry
    tab_all[N] = jnp.full((16, 128), NOBODY, I32)
    xb[BLOCKS - 1, 256:, :] = jnp.zeros((128, 256), BF16)
    sub[:, SUB:, :] = jnp.ones((8, SUB, 1024), BF16)

    @pl.loop(0, BOOKS)
    def _(m):
        words = book_ref[m].astype(F32)
        norm = jnp.sum(words * words, axis=0, keepdims=True)
        first = norm.astype(BF16).astype(F32)
        second = (norm - first).astype(BF16).astype(F32)
        third = norm - first - second
        row = iota((SUB, CODES), 0)
        extra = jnp.where(row == 0, first, jnp.where(row == 1, second, jnp.where(row == 2, third, 0.0)))
        codes[m] = jnp.concatenate([words * -2.0, extra], axis=0).T.astype(BF16)

    r_copy.wait()
    c_copy.wait()

    @pl.loop(0, 4)
    def _(i):
        rows = pl.multiple_of(i * 256, 256)
        for j in range(4):
            rot_t[256 * j : 256 * (j + 1), pl.ds(rows, 256)] = rot[pl.ds(rows, 256), 256 * j : 256 * (j + 1)].T

    @pl.loop(0, 8)
    def _(i):
        rows = pl.multiple_of(i * 256, 256)
        for j in range(4):
            cent_t[256 * j : 256 * (j + 1), pl.ds(rows, 256)] = cent[pl.ds(rows, 256), 256 * j : 256 * (j + 1)].T

    @pl.loop(0, 128)
    def _(t):
        x_copy(t).wait()

    @pl.loop(1, N)
    def _(k):
        tab_copy(k, back(k)).wait_recv()

    lane = iota((16, 128), 1)

    @pl.loop(0, BLOCKS)
    def _(b):
        homes = [tab_all[3 * b + j] + (j << 10) for j in range(3)]
        for s in range(3):
            moved = [pltpu.roll(homes[j], (CAP * (j - s)) % 128, 1) if j != s else homes[j] for j in range(3)]
            found = jnp.where(lane < CAP, moved[0], jnp.where(lane < 2 * CAP, moved[1], moved[2]))
            tab[b, s] = jnp.where(lane < 3 * CAP, found, NOBODY)

    late = jnp.zeros((1, 128), I32)
    first_half = iota((1, 128), 1) < OVER
    for p in range(N // 2):
        left, right = tab_all[2 * p, 11:12, :], tab_all[2 * p + 1, 11:12, :]
        tab_over[p : p + 1, :] = jnp.where(first_half, left, pltpu.roll(right, OVER, 1) + (4 << 8))
        for row in (left, right):
            late = jnp.where(first_half | (((row >> 8) & 63) >= 32), late, 1)
        local_ref[:, 128 * p : 128 * (p + 1)] = tab_over[p : p + 1, :] >> 14
    late = jnp.max(late, axis=1, keepdims=True)
    flag_own[...] = jnp.broadcast_to(late, (8, 128))

    def flag_copy(j, origin):
        return pltpu.make_async_remote_copy(
            src_ref=flag_own,
            dst_ref=flag_all.at[origin],
            send_sem=flag_ss.at[j],
            recv_sem=flag_rs.at[j],
            device_id={"dp": lax.rem(replica + j, DP)},
            device_id_type=MESH,
        )

    for j in range(1, DP):
        flag_copy(j, replica).start()

    def at_owner(b, owner):
        segment = lax.div(owner, 11)
        return tab[b, segment, pl.ds(owner - 11 * segment, 1), :]

    for b in range(BLOCKS):
        local_ref[:, FIRST + 128 * b : FIRST + 128 * (b + 1)] = at_owner(b, me) >> 14

    mine = pl.ds(pl.multiple_of(core * FS, FS), FS)
    for p in range(N // 2):
        entries = tab_over[p : p + 1, :]
        onehot = onehots(iota((256, 128), 0) == (entries & 255))
        groups = jnp.broadcast_to((entries >> 8) & 63, (FS, 128))
        kept = jnp.zeros((FS, 128), F32)
        for j in range(2):
            home = 2 * p + j
            every = dot(xb[home // 3, 128 * (home % 3) : 128 * (home % 3 + 1), :], onehot)
            for g in range(4):
                kept = jnp.where(groups == 4 * j + g, every[FS * g : FS * (g + 1)], kept)
        wide[p // 8, z, x, mine, 128 * (p % 8) : 128 * (p % 8 + 1)] = kept.astype(BF16)

    def along_x(j):
        return (z * 4 + lax.rem(x + j, 4)) * 2 + core

    def along_z(j):
        return (lax.rem(z + j, 4) * 4 + x) * 2 + core

    def ag_copy(slot, part, device):
        return pltpu.make_async_remote_copy(
            src_ref=part,
            dst_ref=part,
            send_sem=ag_ss.at[slot],
            recv_sem=ag_rs.at[slot],
            device_id={"lists": device},
            device_id_type=MESH,
        )

    def phase(number):
        copies = []
        for half in range(2):
            near_one, far_one = (along_x, along_z) if half == 0 else (along_z, along_x)
            for j in range(1, 4):
                slot = 6 * (number - 1) + 3 * half + j - 1
                if number == 1:
                    copies.append((slot, wide.at[half, z, x, mine, :], near_one(j)))
                elif number == 2 and half == 0:
                    copies.append((slot, wide.at[half, z, :, mine, :], far_one(j)))
                elif number == 2:
                    copies.append((slot, wide.at[half, :, x, mine, :], far_one(j)))
            if number == 3:
                copies.append((12 + half, wide.at[half, :, :, mine, :], me + 1 - 2 * core))
        return copies

    def start_phase(number):
        for copy in phase(number):
            ag_copy(*copy).start()

    def wait_phase(number):
        before = lambda v, j: lax.rem(v + 4 - j, 4)
        theirs = pl.ds(pl.multiple_of((1 - core) * FS, FS), FS)
        for half in range(2):
            for j in range(1, 4):
                slot = 6 * (number - 1) + 3 * half + j - 1
                if number == 1:
                    part = wide.at[half, z, before(x, j), mine, :] if half == 0 else wide.at[half, before(z, j), x, mine, :]
                elif number == 2:
                    part = wide.at[half, before(z, j), :, mine, :] if half == 0 else wide.at[half, :, before(x, j), mine, :]
                else:
                    slot, part = 12 + half, wide.at[half, :, :, theirs, :]
                if number < 3 or j == 1:
                    ag_copy(slot, part, peer(1)).wait_recv()

    start_phase(1)

    def vec_copy(part, k, slice_of):
        low, high = PARTS[part]
        return pltpu.make_async_remote_copy(
            src_ref=send.at[k, low:high],
            dst_ref=recv.at[low:high, pl.ds(pl.multiple_of(slice_of * FS, FS), FS), :],
            send_sem=vec_ss.at[part, k],
            recv_sem=vec_rs.at[part, k],
            device_id={"lists": peer(k)},
            device_id_type=MESH,
        )

    def own_copy(part):
        low, high = PARTS[part]
        return pltpu.make_async_copy(
            send.at[0, low:high],
            recv.at[low:high, pl.ds(pl.multiple_of(me * FS, FS), FS), :],
            own_sem.at[part],
        )

    def select_part(part):
        @pl.loop(0, N // 2)
        def _(i):
            owners = [peer(2 * i), peer(2 * i + 1)]
            for b in range(*PARTS[part]):
                entries = jnp.concatenate([at_owner(b, owner) for owner in owners], axis=1)
                every = dot(xb[b], onehots(iota((256, 256), 0) == (entries & 255)))
                groups = jnp.broadcast_to((entries >> 8) & 63, (FS, 256))
                kept = jnp.zeros((FS, 256), F32)
                for g in range(12):
                    kept = jnp.where(groups == g, every[FS * g : FS * (g + 1)], kept)
                kept = kept.astype(BF16)
                send[2 * i, b] = kept[:, :128]
                send[2 * i + 1, b] = kept[:, 128:]

            @pl.when(i == 0)
            def _():
                own_copy(part).start()

            @pl.when(i > 0)
            def _():
                vec_copy(part, 2 * i, me).start()

            vec_copy(part, 2 * i + 1, me).start()

    select_part(0)
    wait_phase(1)
    start_phase(2)
    select_part(1)

    @pl.loop(0, SLOTS // NEAR)
    def _(t):
        lanes = pl.ds(pl.multiple_of(t * NEAR, 128), NEAR)
        onehot = onehots(iota((LISTS, NEAR), 0) == local_ref[:, lanes])
        near[:, lanes] = dot(cent_t[...], onehot).astype(BF16)

        @pl.when(t == 5)
        def _():
            wait_phase(2)
            start_phase(3)

    def encode(width, lanes):
        @pl.loop(0, 2)
        def _(i):
            rows = pl.ds(pl.multiple_of(i * 512, 512), 512)
            turned = dot(rot_t[rows, :], resid[:, :width]).astype(BF16)
            for j in range(8):
                piece = turned[SUB * j : SUB * (j + 1)]
                sub[j, :SUB, :width] = piece
                squares = piece.astype(F32)
                length = jnp.sum(squares * squares, axis=0, keepdims=True)
                least = jnp.min(dot(codes[8 * i + j], sub[j, :, :width]), axis=0, keepdims=True)
                errs[pl.ds(8 * i + j, 1), lanes] = (length + least) * (1.0 / SUB)

    def minus(a, b):
        return (a.astype(F32) - b.astype(F32)).astype(BF16)

    wait_phase(3)

    @pl.loop(0, 2)
    def _(half):
        lanes = pl.ds(pl.multiple_of(half * 1024, 1024), 1024)

        @pl.loop(0, 4)
        def _(i):
            for j in range(4):
                rows = pl.ds(pl.multiple_of(i * 256 + j * 64, 64), 64)
                resid[rows, :] = minus(wide[half, i, j], near[rows, lanes])

        encode(1024, lanes)

    def ret_copy(home, owner):
        return pltpu.make_async_remote_copy(
            src_ref=ret_send.at[home],
            dst_ref=ret_recv.at[owner],
            send_sem=ret_ss.at[home],
            recv_sem=ret_rs.at[owner],
            device_id={"lists": home},
            device_id_type=MESH,
        )

    main_lanes = iota((BOOKS, 128), 1) < 64
    for part, (low, high) in enumerate(PARTS):
        own_copy(part).wait()

        @pl.loop(1, N)
        def _(k):
            vec_copy(part, k, back(k)).wait_recv()

        width, base = 128 * (high - low), FIRST + 128 * low

        @pl.loop(0, 4)
        def _(i):
            rows = pl.ds(pl.multiple_of(i * 256, 256), 256)
            for b in range(low, high):
                resid[rows, 128 * (b - low) : 128 * (b - low + 1)] = minus(
                    recv[b, rows, :], near[rows, FIRST + 128 * b : FIRST + 128 * (b + 1)]
                )

        encode(width, slice(base, base + width))

        for home in range(3 * low, min(3 * high, N)):
            main = errs[:, FIRST + 128 * (home // 3) : FIRST + 128 * (home // 3 + 1)]
            if home % 3:
                main = pltpu.roll(main, 128 - CAP * (home % 3), 1)
            more = errs[:, 128 * (home // 2) : 128 * (home // 2 + 1)]
            if home % 2 == 0:
                more = pltpu.roll(more, OVER, 1)
            ret_send[home] = jnp.where(main_lanes, main, more)

        @pl.loop(3 * low, min(3 * high, N))
        def _(home):
            @pl.when(home == me)
            def _():
                ret_recv[home] = ret_send[home]

            @pl.when(home != me)
            def _():
                ret_copy(home, me).start()

    for j in range(1, DP):
        flag_copy(j, lax.rem(replica + DP - j, DP)).wait_recv()
        late = jnp.maximum(late, flag_all[lax.rem(replica + DP - j, DP)][:1, :1])
    flag_ref[...] = jnp.broadcast_to(late, (8, 128))

    @pl.loop(1, N)
    def _(k):
        ret_copy(me, peer(k)).wait_recv()

    total = jnp.zeros((2 * BOOKS, HOME), F32)
    for t in range(N // 2):
        got = jnp.concatenate([ret_recv[2 * t], ret_recv[2 * t + 1]], axis=1)
        high = got.astype(BF16)
        low = (got - high.astype(F32)).astype(BF16)
        onehot = onehots(iota((256, HOME), 0) + 256 * t == code_ref[...])
        total = total + dot(jnp.concatenate([high, low], axis=0), onehot)
    out_ref[...] = total[:BOOKS] + total[BOOKS:]

    @pl.loop(1, N)
    def _(k):
        tab_copy(k, me).wait_send()
        ret_copy(peer(k), me).wait_send()
        for part in range(len(PARTS)):
            vec_copy(part, k, me).wait_send()

    for number in range(1, 4):
        for copy in phase(number):
            ag_copy(*copy).wait_send()
    for j in range(1, DP):
        flag_copy(j, replica).wait_send()


def fast(embeddings, assign, list_slot, centroids, rotation, codebook):
    vmem = pl.BlockSpec(memory_space=pltpu.VMEM)
    hbm = pl.BlockSpec(memory_space=pl.ANY)
    dma = pltpu.SemaphoreType.DMA
    return pl.pallas_call(
        kernel,
        out_shape=(jax.ShapeDtypeStruct((BOOKS, HOME), F32), jax.ShapeDtypeStruct((8, 128), I32)),
        in_specs=[hbm, vmem, vmem, hbm, hbm, vmem],
        out_specs=(vmem, vmem),
        scratch_shapes=[
            pltpu.VMEM((BLOCKS, 384, 256), BF16),
            pltpu.VMEM((N, BLOCKS, FS, 128), BF16),
            pltpu.VMEM((BLOCKS, D, 128), BF16),
            pltpu.VMEM((2, 4, 4, 2 * FS, 1024), BF16),
            pltpu.VMEM((D, SLOTS), BF16),
            pltpu.VMEM((LISTS, D), BF16),
            pltpu.VMEM((D, LISTS), BF16),
            pltpu.VMEM((D, D), BF16),
            pltpu.VMEM((D, D), BF16),
            pltpu.VMEM((BOOKS, CODES, 2 * SUB), BF16),
            pltpu.VMEM((16, 128), I32),
            pltpu.VMEM((N + 1, 16, 128), I32),
            pltpu.VMEM((BLOCKS, 3, 16, 128), I32),
            pltpu.VMEM((N // 2, 128), I32),
            pltpu.VMEM((1, SLOTS), I32),
            pltpu.VMEM((D, 1024), BF16),
            pltpu.VMEM((8, 2 * SUB, 1024), BF16),
            pltpu.VMEM((BOOKS, SLOTS), F32),
            pltpu.VMEM((1, HOME), I32),
            pltpu.VMEM((N, BOOKS, 128), F32),
            pltpu.VMEM((N, BOOKS, 128), F32),
            pltpu.VMEM((8, 128), I32),
            pltpu.VMEM((DP, 8, 128), I32),
            dma((128,)), dma, dma, dma((len(PARTS),)),
            dma((N,)), dma((N,)),
            dma((len(PARTS), N)), dma((len(PARTS), N)),
            dma((N,)), dma((N,)),
            dma((14,)), dma((14,)),
            dma((DP,)), dma((DP,)),
        ],
        compiler_params=pltpu.CompilerParams(
            collective_id=0, has_side_effects=True, vmem_limit_bytes=58 * 2**20
        ),
        name="encode",
    )(
        embeddings.T,
        assign.reshape(1, HOME),
        list_slot.reshape(512, 128),
        centroids,
        rotation.reshape(D, D),
        codebook.transpose(0, 2, 1),
    )


def route_rows(assigned, list_slot, list_width, owner_count):
    slot_index = jnp.take(list_slot, assigned)
    target = slot_index // list_width
    local_row = slot_index - target * list_width
    onehot = (target[..., None] == jnp.arange(owner_count, dtype=jnp.int32)).astype(jnp.int32)
    position = jnp.sum(jnp.cumsum(onehot, axis=-2) * onehot, axis=-1) - 1
    return (target, local_row, position)


def encode_rows(received, row_ids, centroids, rotation, codebook, code_norms):
    senders, slot_count, model_width = received.shape
    flattened = received.reshape(senders * slot_count, model_width)
    centre_rows = jnp.take(centroids, row_ids.reshape(-1), axis=0)
    residual = (flattened.astype(jnp.float32) - centre_rows.astype(jnp.float32)).astype(
        jnp.bfloat16
    )
    rotated = jnp.dot(residual, rotation[0], preferred_element_type=jnp.float32).astype(
        jnp.bfloat16
    )
    book_count, centres, sub_width = codebook.shape

    def one_book(book_index):
        subspace = lax.dynamic_slice_in_dim(rotated, book_index * sub_width, sub_width, 1)
        codewords = lax.dynamic_index_in_dim(codebook, book_index, 0, keepdims=False)
        norm_row = lax.dynamic_index_in_dim(code_norms, book_index, 0, keepdims=False)
        products = lax.dot_general(
            subspace, codewords, (((1,), (1,)), ((), ())), preferred_element_type=jnp.float32
        )
        lengths = jnp.sum(jnp.square(subspace.astype(jnp.float32)), axis=1)
        distance = lengths[:, None] + norm_row[None, :] - 2.0 * products
        return jnp.min(distance, axis=1) / sub_width

    errors = lax.map(one_book, jnp.arange(book_count, dtype=jnp.int32))
    errors = errors.reshape(book_count, senders, slot_count).transpose(1, 0, 2)
    return lax.all_to_all(errors, "lists", split_axis=0, concat_axis=0, tiled=True)


def general(embeddings, assign, list_slot, centroids, rotation, codebook):
    owner_count = lax.axis_size("lists")
    list_width = centroids.shape[0]
    home_rows = assign.shape[0]
    capacity = 3 * home_rows // owner_count
    model_width = rotation.shape[1]
    code_norms = jnp.sum(jnp.square(codebook.astype(jnp.float32)), axis=2)
    target, local_row, position = route_rows(assign, list_slot, list_width, owner_count)
    vectors = lax.all_to_all(embeddings, "lists", split_axis=0, concat_axis=1, tiled=True)
    outgoing = (
        jnp.zeros((owner_count, capacity, model_width), jnp.bfloat16)
        .at[target, position]
        .set(vectors)
    )
    row_ids = jnp.zeros((owner_count, capacity), jnp.int32).at[target, position].set(local_row)
    returned = encode_rows(
        lax.all_to_all(outgoing, "lists", split_axis=0, concat_axis=0, tiled=True),
        lax.all_to_all(row_ids, "lists", split_axis=0, concat_axis=0, tiled=True),
        centroids,
        rotation,
        codebook,
        code_norms,
    )
    return jnp.transpose(returned, (1, 0, 2))[:, target, position]


def shards(*arrays):
    errors, flag = fast(*arrays)
    return lax.cond(flag[0, 0] > 0, lambda: general(*arrays), lambda: errors)


def solution(mesh):
    placed = (
        P("dp", "lists"),
        P(("dp", "lists")),
        P(),
        P("lists", None),
        P("lists", None, None),
        P(),
    )
    return jax.shard_map(
        shards, mesh=mesh, in_specs=placed, out_specs=P(None, ("dp", "lists")), check_vma=False
    )
```

```python
import jax
import jax.numpy as jnp
from jax import lax
from jax.experimental import pallas as pl
from jax.experimental.pallas import tpu as pltpu
from jax.sharding import PartitionSpec as P

MESH = pl.DeviceIdType.MESH
F32 = jnp.float32
BF16 = jnp.bfloat16
I32 = jnp.int32

N = 32
DP = 4
HOME = 1024
D = 1024
FS = 32
LISTS = 2048
BOOKS, CODES, SUB = 16, 256, 64
CAP = 42
OVER = 64
BLOCKS = 11
PARTS = ((0, 6), (6, 11))
FIRST = N * OVER
SLOTS = FIRST + 128 * BLOCKS
NEAR = 512
PHASE = 6
NEARS = -(-SLOTS // NEAR)
NOBODY = 32 << 8


def dot(a, b):
    return jnp.dot(a, b, preferred_element_type=F32)


def iota(shape, dim):
    return lax.broadcasted_iota(I32, shape, dim)


def onehots(mask):
    return mask.astype(F32).astype(BF16)


def routes(assign_ref, slots_ref):
    assigned = assign_ref[...]
    table = slots_ref[...].astype(F32).T.astype(I32)
    table = jnp.concatenate([table >> 8, table & 255], axis=0).astype(F32).astype(BF16)
    picked = dot(table, onehots(iota((512, HOME), 0) == (assigned >> 7)))
    low = iota((128, HOME), 0) == (assigned & 127)
    upper = jnp.sum(jnp.where(low, picked[:128], 0.0), axis=0, keepdims=True)
    lower = jnp.sum(jnp.where(low, picked[128:], 0.0), axis=0, keepdims=True)
    slot = upper.astype(I32) * 256 + lower.astype(I32)
    target, local = slot >> 11, slot & (LISTS - 1)
    mine = iota((N, HOME), 0) == target
    before = onehots(iota((HOME, HOME), 0) < iota((HOME, HOME), 1))
    ahead = dot(onehots(mine), before)
    rank = jnp.sum(jnp.where(mine, ahead, 0.0), axis=0, keepdims=True).astype(I32)
    over = rank >= CAP
    over_rank = dot(jnp.broadcast_to(onehots(over), (8, HOME)), before)[:1].astype(I32)
    segment = (target >= 11).astype(I32) + (target >= 22).astype(I32)
    row = jnp.where(over, 11, target - 11 * segment)
    lane = jnp.where(over, over_rank, CAP * segment + rank)
    mine = iota((16, HOME), 0) == row
    place = onehots(iota((128, HOME), 0) == lane)
    vector = iota((1, HOME), 1)
    fields = [vector & 255, vector >> 8, local & 255, local >> 8, jnp.ones_like(vector)]
    planes = [jnp.where(mine, field.astype(F32), 0.0) for field in fields]
    planes = jnp.concatenate(planes, axis=0).astype(BF16)
    held = lax.dot_general(planes, place, (((1,), (1,)), ((), ())), preferred_element_type=F32).astype(I32)
    index, group, local_low, local_high, valid = (held[16 * j : 16 * (j + 1)] for j in range(5))
    entry = index + (group << 8) + (local_low << 14) + (local_high << 22)
    entry = jnp.where(valid > 0, entry, NOBODY)
    return target * 128 + jnp.where(over, 64 + over_rank, rank), entry


def kernel(
    emb_ref, assign_ref, slots_ref, cent_ref, rot_ref, book_ref, out_ref, flag_ref,
    xb, send, recv, wide, near, cent, cent_t, rot, rot_t, codes, tab_own, tab_all, tab, tab_over, local_ref,
    resid, sub, errs, code_ref, ret_send, ret_recv, flag_own, flag_all,
    x_sem, c_sem, r_sem, own_sem, tab_ss, tab_rs, vec_ss, vec_rs, ret_ss, ret_rs, ag_ss, ag_rs, flag_ss, flag_rs,
):
    me = lax.axis_index("lists")
    replica = lax.axis_index("dp")
    core = lax.rem(me, 2)
    x = lax.rem(lax.div(me, 2), 4)
    z = lax.div(me, 8)

    def peer(k):
        return lax.rem(me + k, N)

    def back(k):
        return lax.rem(me + N - k, N)

    barrier = pltpu.get_barrier_semaphore()

    @pl.loop(1, N)
    def _(k):
        pl.semaphore_signal(barrier, inc=1, device_id={"lists": peer(k)}, device_id_type=MESH)

    for j in range(1, DP):
        other = lax.rem(replica + j, DP)
        pl.semaphore_signal(barrier, inc=1, device_id={"dp": other}, device_id_type=MESH)

    def x_copy(t):
        block = lax.div(t, 12)
        group = t - block * 12
        return pltpu.make_async_copy(
            emb_ref.at[:, pl.ds(pl.multiple_of(t * 256, 256), 256)],
            xb.at[block, pl.ds(pl.multiple_of(group * FS, FS), FS), :],
            x_sem.at[t],
        )

    @pl.loop(0, 128)
    def _(t):
        x_copy(t).start()

    c_copy = pltpu.make_async_copy(cent_ref, cent, c_sem)
    r_copy = pltpu.make_async_copy(rot_ref, rot, r_sem)
    c_copy.start()
    r_copy.start()

    code, entry = routes(assign_ref, slots_ref)
    code_ref[...] = code
    tab_own[...] = entry

    pl.semaphore_wait(barrier, N - 1 + DP - 1)

    def tab_copy(k, home):
        return pltpu.make_async_remote_copy(
            src_ref=tab_own,
            dst_ref=tab_all.at[home],
            send_sem=tab_ss.at[k],
            recv_sem=tab_rs.at[k],
            device_id={"lists": peer(k)},
            device_id_type=MESH,
        )

    @pl.loop(1, N)
    def _(k):
        tab_copy(k, me).start()

    tab_all[me] = entry
    tab_all[N] = jnp.full((16, 128), NOBODY, I32)
    xb[BLOCKS - 1, 256:, :] = jnp.zeros((128, 256), BF16)
    sub[:, SUB:, :] = jnp.ones((8, SUB, 1024), BF16)

    @pl.loop(0, BOOKS)
    def _(m):
        words = book_ref[m].astype(F32)
        norm = jnp.sum(words * words, axis=0, keepdims=True)
        first = norm.astype(BF16).astype(F32)
        second = (norm - first).astype(BF16).astype(F32)
        third = norm - first - second
        row = iota((SUB, CODES), 0)
        extra = jnp.where(row == 0, first, jnp.where(row == 1, second, jnp.where(row == 2, third, 0.0)))
        codes[m] = jnp.concatenate([words * -2.0, extra], axis=0).T.astype(BF16)

    r_copy.wait()
    c_copy.wait()

    @pl.loop(0, 4)
    def _(i):
        rows = pl.multiple_of(i * 256, 256)
        for j in range(4):
            rot_t[256 * j : 256 * (j + 1), pl.ds(rows, 256)] = rot[pl.ds(rows, 256), 256 * j : 256 * (j + 1)].T

    @pl.loop(0, 8)
    def _(i):
        rows = pl.multiple_of(i * 256, 256)
        for j in range(4):
            cent_t[256 * j : 256 * (j + 1), pl.ds(rows, 256)] = cent[pl.ds(rows, 256), 256 * j : 256 * (j + 1)].T

    @pl.loop(0, 128)
    def _(t):
        x_copy(t).wait()

    @pl.loop(1, N)
    def _(k):
        tab_copy(k, back(k)).wait_recv()

    lane = iota((16, 128), 1)

    @pl.loop(0, BLOCKS)
    def _(b):
        homes = [tab_all[3 * b + j] + (j << 10) for j in range(3)]
        for s in range(3):
            moved = [pltpu.roll(homes[j], (CAP * (j - s)) % 128, 1) if j != s else homes[j] for j in range(3)]
            found = jnp.where(lane < CAP, moved[0], jnp.where(lane < 2 * CAP, moved[1], moved[2]))
            tab[b, s] = jnp.where(lane < 3 * CAP, found, NOBODY)

    late = jnp.zeros((1, 128), I32)
    first_half = iota((1, 128), 1) < OVER
    for p in range(N // 2):
        left, right = tab_all[2 * p, 11:12, :], tab_all[2 * p + 1, 11:12, :]
        tab_over[p : p + 1, :] = jnp.where(first_half, left, pltpu.roll(right, OVER, 1) + (4 << 8))
        for row in (left, right):
            late = jnp.where(first_half | (((row >> 8) & 63) >= 32), late, 1)
        local_ref[:, 128 * p : 128 * (p + 1)] = tab_over[p : p + 1, :] >> 14
    late = jnp.max(late, axis=1, keepdims=True)
    flag_own[...] = jnp.broadcast_to(late, (8, 128))

    def flag_copy(j, origin):
        return pltpu.make_async_remote_copy(
            src_ref=flag_own,
            dst_ref=flag_all.at[origin],
            send_sem=flag_ss.at[j],
            recv_sem=flag_rs.at[j],
            device_id={"dp": lax.rem(replica + j, DP)},
            device_id_type=MESH,
        )

    for j in range(1, DP):
        flag_copy(j, replica).start()

    def at_owner(b, owner):
        segment = lax.div(owner, 11)
        return tab[b, segment, pl.ds(owner - 11 * segment, 1), :]

    local_ref[:, SLOTS:] = jnp.zeros((1, NEARS * NEAR - SLOTS), I32)
    for b in range(BLOCKS):
        local_ref[:, FIRST + 128 * b : FIRST + 128 * (b + 1)] = at_owner(b, me) >> 14

    mine = pl.ds(pl.multiple_of(core * FS, FS), FS)
    for p in range(N // 2):
        entries = tab_over[p : p + 1, :]
        onehot = onehots(iota((256, 128), 0) == (entries & 255))
        groups = jnp.broadcast_to((entries >> 8) & 63, (FS, 128))
        kept = jnp.zeros((FS, 128), F32)
        for j in range(2):
            home = 2 * p + j
            every = dot(xb[home // 3, 128 * (home % 3) : 128 * (home % 3 + 1), :], onehot)
            for g in range(4):
                kept = jnp.where(groups == 4 * j + g, every[FS * g : FS * (g + 1)], kept)
        wide[p // 8, z, x, mine, 128 * (p % 8) : 128 * (p % 8 + 1)] = kept.astype(BF16)

    def along_x(j):
        return (z * 4 + lax.rem(x + j, 4)) * 2 + core

    def along_z(j):
        return (lax.rem(z + j, 4) * 4 + x) * 2 + core

    def ag_copy(slot, part, device):
        return pltpu.make_async_remote_copy(
            src_ref=part,
            dst_ref=part,
            send_sem=ag_ss.at[slot],
            recv_sem=ag_rs.at[slot],
            device_id={"lists": device},
            device_id_type=MESH,
        )

    def phase(number):
        copies = []
        for half in range(2):
            near_one, far_one = (along_x, along_z) if half == 0 else (along_z, along_x)
            for j in range(1, 4):
                slot = 6 * (number - 1) + 3 * half + j - 1
                if number == 1:
                    copies.append((slot, wide.at[half, z, x, mine, :], near_one(j)))
                elif number == 2 and half == 0:
                    copies.append((slot, wide.at[half, z, :, mine, :], far_one(j)))
                elif number == 2:
                    copies.append((slot, wide.at[half, :, x, mine, :], far_one(j)))
            if number == 3:
                copies.append((12 + half, wide.at[half, :, :, mine, :], me + 1 - 2 * core))
        return copies

    def start_phase(number):
        for copy in phase(number):
            ag_copy(*copy).start()

    def wait_phase(number):
        before = lambda v, j: lax.rem(v + 4 - j, 4)
        theirs = pl.ds(pl.multiple_of((1 - core) * FS, FS), FS)
        for half in range(2):
            for j in range(1, 4):
                slot = 6 * (number - 1) + 3 * half + j - 1
                if number == 1:
                    part = wide.at[half, z, before(x, j), mine, :] if half == 0 else wide.at[half, before(z, j), x, mine, :]
                elif number == 2:
                    part = wide.at[half, before(z, j), :, mine, :] if half == 0 else wide.at[half, :, before(x, j), mine, :]
                else:
                    slot, part = 12 + half, wide.at[half, :, :, theirs, :]
                if number < 3 or j == 1:
                    ag_copy(slot, part, peer(1)).wait_recv()

    start_phase(1)

    def across(i):
        chip = lax.rem(z + lax.rem(i, 4), 4) * 4 + lax.rem(x + lax.rem(lax.div(i, 4) + i, 4), 4)
        return [chip * 2 + core, chip * 2 + 1 - core]

    def vec_copy(part, k, owner, slice_of):
        low, high = PARTS[part]
        return pltpu.make_async_remote_copy(
            src_ref=send.at[k, low:high],
            dst_ref=recv.at[low:high, pl.ds(pl.multiple_of(slice_of * FS, FS), FS), :],
            send_sem=vec_ss.at[part, k],
            recv_sem=vec_rs.at[part, slice_of],
            device_id={"lists": owner},
            device_id_type=MESH,
        )

    def own_copy(part):
        low, high = PARTS[part]
        return pltpu.make_async_copy(
            send.at[0, low:high],
            recv.at[low:high, pl.ds(pl.multiple_of(me * FS, FS), FS), :],
            own_sem.at[part],
        )

    def select_part(part):
        @pl.loop(0, N // 2)
        def _(i):
            owners = across(i)
            for b in range(*PARTS[part]):
                entries = jnp.concatenate([at_owner(b, owner) for owner in owners], axis=1)
                every = dot(xb[b], onehots(iota((256, 256), 0) == (entries & 255)))
                groups = jnp.broadcast_to((entries >> 8) & 63, (FS, 256))
                kept = jnp.zeros((FS, 256), F32)
                for g in range(12):
                    kept = jnp.where(groups == g, every[FS * g : FS * (g + 1)], kept)
                kept = kept.astype(BF16)
                send[2 * i, b] = kept[:, :128]
                send[2 * i + 1, b] = kept[:, 128:]

            @pl.when(i == 0)
            def _():
                own_copy(part).start()

            @pl.when(i > 0)
            def _():
                vec_copy(part, 2 * i, owners[0], me).start()

            vec_copy(part, 2 * i + 1, owners[1], me).start()

    select_part(0)
    wait_phase(1)
    start_phase(2)
    select_part(1)

    @pl.loop(0, NEARS)
    def _(t):
        lanes = pl.ds(pl.multiple_of(t * NEAR, 128), NEAR)
        onehot = onehots(iota((LISTS, NEAR), 0) == local_ref[:, lanes])
        near[:, lanes] = dot(cent_t[...], onehot).astype(BF16)

        @pl.when(t == PHASE)
        def _():
            wait_phase(2)
            start_phase(3)

    def encode(width, lanes):
        @pl.loop(0, 2)
        def _(i):
            rows = pl.ds(pl.multiple_of(i * 512, 512), 512)
            turned = dot(rot_t[rows, :], resid[:, :width]).astype(BF16)
            for j in range(8):
                piece = turned[SUB * j : SUB * (j + 1)]
                sub[j, :SUB, :width] = piece
                squares = piece.astype(F32)
                length = jnp.sum(squares * squares, axis=0, keepdims=True)
                least = jnp.min(dot(codes[8 * i + j], sub[j, :, :width]), axis=0, keepdims=True)
                errs[pl.ds(8 * i + j, 1), lanes] = (length + least) * (1.0 / SUB)

    def minus(a, b):
        return (a.astype(F32) - b.astype(F32)).astype(BF16)

    def ret_copy(home, owner):
        return pltpu.make_async_remote_copy(
            src_ref=ret_send.at[home],
            dst_ref=ret_recv.at[owner],
            send_sem=ret_ss.at[home],
            recv_sem=ret_rs.at[owner],
            device_id={"lists": home},
            device_id_type=MESH,
        )

    def overflow():
        wait_phase(3)

        @pl.loop(0, 2)
        def _(half):
            lanes = pl.ds(pl.multiple_of(half * 1024, 1024), 1024)

            @pl.loop(0, 4)
            def _(i):
                for j in range(4):
                    rows = pl.ds(pl.multiple_of(i * 256 + j * 64, 64), 64)
                    resid[rows, :] = minus(wide[half, i, j], near[rows, lanes])

            encode(1024, lanes)

    main_lanes = iota((BOOKS, 128), 1) < 64
    def main(part):
        low, high = PARTS[part]
        own_copy(part).wait()

        @pl.loop(1, N)
        def _(k):
            vec_copy(part, k, peer(1), back(k)).wait_recv()

        width, base = 128 * (high - low), FIRST + 128 * low

        @pl.loop(0, 4)
        def _(i):
            rows = pl.ds(pl.multiple_of(i * 256, 256), 256)
            for b in range(low, high):
                resid[rows, 128 * (b - low) : 128 * (b - low + 1)] = minus(
                    recv[b, rows, :], near[rows, FIRST + 128 * b : FIRST + 128 * (b + 1)]
                )

        encode(width, slice(base, base + width))

    def give_back(part):
        low, high = PARTS[part]
        for home in range(3 * low, min(3 * high, N)):
            least = errs[:, FIRST + 128 * (home // 3) : FIRST + 128 * (home // 3 + 1)]
            if home % 3:
                least = pltpu.roll(least, 128 - CAP * (home % 3), 1)
            more = errs[:, 128 * (home // 2) : 128 * (home // 2 + 1)]
            if home % 2 == 0:
                more = pltpu.roll(more, OVER, 1)
            ret_send[home] = jnp.where(main_lanes, least, more)

        @pl.loop(3 * low, min(3 * high, N))
        def _(home):
            @pl.when(home == me)
            def _():
                ret_recv[home] = ret_send[home]

            @pl.when(home != me)
            def _():
                ret_copy(home, me).start()

    main(0)
    overflow()
    give_back(0)
    main(1)
    give_back(1)

    for j in range(1, DP):
        flag_copy(j, lax.rem(replica + DP - j, DP)).wait_recv()
        late = jnp.maximum(late, flag_all[lax.rem(replica + DP - j, DP)][:1, :1])
    flag_ref[...] = jnp.broadcast_to(late, (8, 128))

    @pl.loop(1, N)
    def _(k):
        ret_copy(me, peer(k)).wait_recv()

    total = jnp.zeros((2 * BOOKS, HOME), F32)
    for t in range(N // 2):
        got = jnp.concatenate([ret_recv[2 * t], ret_recv[2 * t + 1]], axis=1)
        high = got.astype(BF16)
        low = (got - high.astype(F32)).astype(BF16)
        onehot = onehots(iota((256, HOME), 0) + 256 * t == code_ref[...])
        total = total + dot(jnp.concatenate([high, low], axis=0), onehot)
    out_ref[...] = total[:BOOKS] + total[BOOKS:]

    @pl.loop(1, N)
    def _(k):
        tab_copy(k, me).wait_send()
        ret_copy(peer(k), me).wait_send()
        for part in range(len(PARTS)):
            vec_copy(part, k, peer(1), me).wait_send()

    for number in range(1, 4):
        for copy in phase(number):
            ag_copy(*copy).wait_send()
    for j in range(1, DP):
        flag_copy(j, replica).wait_send()


def fast(embeddings, assign, list_slot, centroids, rotation, codebook):
    vmem = pl.BlockSpec(memory_space=pltpu.VMEM)
    hbm = pl.BlockSpec(memory_space=pl.ANY)
    dma = pltpu.SemaphoreType.DMA
    return pl.pallas_call(
        kernel,
        out_shape=(jax.ShapeDtypeStruct((BOOKS, HOME), F32), jax.ShapeDtypeStruct((8, 128), I32)),
        in_specs=[hbm, vmem, vmem, hbm, hbm, vmem],
        out_specs=(vmem, vmem),
        scratch_shapes=[
            pltpu.VMEM((BLOCKS, 384, 256), BF16),
            pltpu.VMEM((N, BLOCKS, FS, 128), BF16),
            pltpu.VMEM((BLOCKS, D, 128), BF16),
            pltpu.VMEM((2, 4, 4, 2 * FS, 1024), BF16),
            pltpu.VMEM((D, NEARS * NEAR), BF16),
            pltpu.VMEM((LISTS, D), BF16),
            pltpu.VMEM((D, LISTS), BF16),
            pltpu.VMEM((D, D), BF16),
            pltpu.VMEM((D, D), BF16),
            pltpu.VMEM((BOOKS, CODES, 2 * SUB), BF16),
            pltpu.VMEM((16, 128), I32),
            pltpu.VMEM((N + 1, 16, 128), I32),
            pltpu.VMEM((BLOCKS, 3, 16, 128), I32),
            pltpu.VMEM((N // 2, 128), I32),
            pltpu.VMEM((1, NEARS * NEAR), I32),
            pltpu.VMEM((D, 1024), BF16),
            pltpu.VMEM((8, 2 * SUB, 1024), BF16),
            pltpu.VMEM((BOOKS, SLOTS), F32),
            pltpu.VMEM((1, HOME), I32),
            pltpu.VMEM((N, BOOKS, 128), F32),
            pltpu.VMEM((N, BOOKS, 128), F32),
            pltpu.VMEM((8, 128), I32),
            pltpu.VMEM((DP, 8, 128), I32),
            dma((128,)), dma, dma, dma((len(PARTS),)),
            dma((N,)), dma((N,)),
            dma((len(PARTS), N)), dma((len(PARTS), N)),
            dma((N,)), dma((N,)),
            dma((14,)), dma((14,)),
            dma((DP,)), dma((DP,)),
        ],
        compiler_params=pltpu.CompilerParams(
            collective_id=0, has_side_effects=True, vmem_limit_bytes=58 * 2**20
        ),
        name="encode",
    )(
        embeddings.T,
        assign.reshape(1, HOME),
        list_slot.reshape(512, 128),
        centroids,
        rotation.reshape(D, D),
        codebook.transpose(0, 2, 1),
    )


def route_rows(assigned, list_slot, list_width, owner_count):
    slot_index = jnp.take(list_slot, assigned)
    target = slot_index // list_width
    local_row = slot_index - target * list_width
    onehot = (target[..., None] == jnp.arange(owner_count, dtype=jnp.int32)).astype(jnp.int32)
    position = jnp.sum(jnp.cumsum(onehot, axis=-2) * onehot, axis=-1) - 1
    return (target, local_row, position)


def encode_rows(received, row_ids, centroids, rotation, codebook, code_norms):
    senders, slot_count, model_width = received.shape
    flattened = received.reshape(senders * slot_count, model_width)
    centre_rows = jnp.take(centroids, row_ids.reshape(-1), axis=0)
    residual = (flattened.astype(jnp.float32) - centre_rows.astype(jnp.float32)).astype(
        jnp.bfloat16
    )
    rotated = jnp.dot(residual, rotation[0], preferred_element_type=jnp.float32).astype(
        jnp.bfloat16
    )
    book_count, centres, sub_width = codebook.shape

    def one_book(book_index):
        subspace = lax.dynamic_slice_in_dim(rotated, book_index * sub_width, sub_width, 1)
        codewords = lax.dynamic_index_in_dim(codebook, book_index, 0, keepdims=False)
        norm_row = lax.dynamic_index_in_dim(code_norms, book_index, 0, keepdims=False)
        products = lax.dot_general(
            subspace, codewords, (((1,), (1,)), ((), ())), preferred_element_type=jnp.float32
        )
        lengths = jnp.sum(jnp.square(subspace.astype(jnp.float32)), axis=1)
        distance = lengths[:, None] + norm_row[None, :] - 2.0 * products
        return jnp.min(distance, axis=1) / sub_width

    errors = lax.map(one_book, jnp.arange(book_count, dtype=jnp.int32))
    errors = errors.reshape(book_count, senders, slot_count).transpose(1, 0, 2)
    return lax.all_to_all(errors, "lists", split_axis=0, concat_axis=0, tiled=True)


def general(embeddings, assign, list_slot, centroids, rotation, codebook):
    owner_count = lax.axis_size("lists")
    list_width = centroids.shape[0]
    home_rows = assign.shape[0]
    capacity = 3 * home_rows // owner_count
    model_width = rotation.shape[1]
    code_norms = jnp.sum(jnp.square(codebook.astype(jnp.float32)), axis=2)
    target, local_row, position = route_rows(assign, list_slot, list_width, owner_count)
    vectors = lax.all_to_all(embeddings, "lists", split_axis=0, concat_axis=1, tiled=True)
    outgoing = (
        jnp.zeros((owner_count, capacity, model_width), jnp.bfloat16)
        .at[target, position]
        .set(vectors)
    )
    row_ids = jnp.zeros((owner_count, capacity), jnp.int32).at[target, position].set(local_row)
    returned = encode_rows(
        lax.all_to_all(outgoing, "lists", split_axis=0, concat_axis=0, tiled=True),
        lax.all_to_all(row_ids, "lists", split_axis=0, concat_axis=0, tiled=True),
        centroids,
        rotation,
        codebook,
        code_norms,
    )
    return jnp.transpose(returned, (1, 0, 2))[:, target, position]


def shards(*arrays):
    errors, flag = fast(*arrays)
    return lax.cond(flag[0, 0] > 0, lambda: general(*arrays), lambda: errors)


def solution(mesh):
    placed = (
        P("dp", "lists"),
        P(("dp", "lists")),
        P(),
        P("lists", None),
        P("lists", None, None),
        P(),
    )
    return jax.shard_map(
        shards, mesh=mesh, in_specs=placed, out_specs=P(None, ("dp", "lists")), check_vma=False
    )
```

```python
import jax
import jax.numpy as jnp
from jax import lax
from jax.experimental import pallas as pl
from jax.experimental.pallas import tpu as pltpu
from jax.sharding import PartitionSpec as P

MESH = pl.DeviceIdType.MESH
F32 = jnp.float32
BF16 = jnp.bfloat16
I32 = jnp.int32

N = 32
DP = 4
HOME = 1024
D = 1024
FS = 32
LISTS = 2048
BOOKS, CODES, SUB = 16, 256, 64
CAP = 42
OVER = 64
BLOCKS = 11
PARTS = ((0, 4), (4, 8), (8, 11))
FIRST = N * OVER
SLOTS = FIRST + 128 * BLOCKS
NEAR = 512
GROUP = 4
EARLY = 2
PHASE = 2
LATER = {1: 1, 2: 3}
NEARS = -(-SLOTS // NEAR)
NOBODY = 32 << 8


def dot(a, b):
    return jnp.dot(a, b, preferred_element_type=F32)


def iota(shape, dim):
    return lax.broadcasted_iota(I32, shape, dim)


def onehots(mask):
    return mask.astype(F32).astype(BF16)


def routes(assign_ref, slots_ref):
    assigned = assign_ref[...]
    table = slots_ref[...].astype(F32).T.astype(I32)
    table = jnp.concatenate([table >> 8, table & 255], axis=0).astype(F32).astype(BF16)
    picked = dot(table, onehots(iota((512, HOME), 0) == (assigned >> 7)))
    low = iota((128, HOME), 0) == (assigned & 127)
    upper = jnp.sum(jnp.where(low, picked[:128], 0.0), axis=0, keepdims=True)
    lower = jnp.sum(jnp.where(low, picked[128:], 0.0), axis=0, keepdims=True)
    slot = upper.astype(I32) * 256 + lower.astype(I32)
    target, local = slot >> 11, slot & (LISTS - 1)
    mine = iota((N, HOME), 0) == target
    before = onehots(iota((HOME, HOME), 0) < iota((HOME, HOME), 1))
    ahead = dot(onehots(mine), before)
    rank = jnp.sum(jnp.where(mine, ahead, 0.0), axis=0, keepdims=True).astype(I32)
    over = rank >= CAP
    over_rank = dot(jnp.broadcast_to(onehots(over), (8, HOME)), before)[:1].astype(I32)
    segment = (target >= 11).astype(I32) + (target >= 22).astype(I32)
    row = jnp.where(over, 11, target - 11 * segment)
    lane = jnp.where(over, over_rank, CAP * segment + rank)
    mine = iota((16, HOME), 0) == row
    place = onehots(iota((128, HOME), 0) == lane)
    vector = iota((1, HOME), 1)
    fields = [vector & 255, vector >> 8, local & 255, local >> 8, jnp.ones_like(vector)]
    planes = [jnp.where(mine, field.astype(F32), 0.0) for field in fields]
    planes = jnp.concatenate(planes, axis=0).astype(BF16)
    held = lax.dot_general(planes, place, (((1,), (1,)), ((), ())), preferred_element_type=F32).astype(I32)
    index, group, local_low, local_high, valid = (held[16 * j : 16 * (j + 1)] for j in range(5))
    entry = index + (group << 8) + (local_low << 14) + (local_high << 22)
    entry = jnp.where(valid > 0, entry, NOBODY)
    return target * 128 + jnp.where(over, 64 + over_rank, rank), entry


def kernel(
    emb_ref, assign_ref, slots_ref, cent_ref, rot_ref, book_ref, out_ref, flag_ref,
    xb, send, recv, wide, near, cent, cent_t, rot, rot_t, codes, tab_own, tab_all, tab, tab_over, local_ref,
    resid, sub, errs, code_ref, ret_send, ret_recv, flag_own, flag_all,
    x_sem, c_sem, r_sem, own_sem, tab_ss, tab_rs, vec_ss, vec_rs, ret_ss, ret_rs, ag_ss, ag_rs, flag_ss, flag_rs,
):
    me = lax.axis_index("lists")
    replica = lax.axis_index("dp")
    core = lax.rem(me, 2)
    x = lax.rem(lax.div(me, 2), 4)
    z = lax.div(me, 8)

    def peer(k):
        return lax.rem(me + k, N)

    def back(k):
        return lax.rem(me + N - k, N)

    barrier = pltpu.get_barrier_semaphore()

    @pl.loop(1, N)
    def _(k):
        pl.semaphore_signal(barrier, inc=1, device_id={"lists": peer(k)}, device_id_type=MESH)

    for j in range(1, DP):
        other = lax.rem(replica + j, DP)
        pl.semaphore_signal(barrier, inc=1, device_id={"dp": other}, device_id_type=MESH)

    def x_copy(t):
        block = lax.div(t, 12)
        group = t - block * 12
        return pltpu.make_async_copy(
            emb_ref.at[:, pl.ds(pl.multiple_of(t * 256, 256), 256)],
            xb.at[block, pl.ds(pl.multiple_of(group * FS, FS), FS), :],
            x_sem.at[t],
        )

    @pl.loop(0, 128)
    def _(t):
        x_copy(t).start()

    c_copy = pltpu.make_async_copy(cent_ref, cent, c_sem)
    r_copy = pltpu.make_async_copy(rot_ref, rot, r_sem)
    c_copy.start()
    r_copy.start()

    code, entry = routes(assign_ref, slots_ref)
    code_ref[...] = code
    tab_own[...] = entry

    pl.semaphore_wait(barrier, N - 1 + DP - 1)

    def tab_copy(k, home):
        return pltpu.make_async_remote_copy(
            src_ref=tab_own,
            dst_ref=tab_all.at[home],
            send_sem=tab_ss.at[k],
            recv_sem=tab_rs.at[k],
            device_id={"lists": peer(k)},
            device_id_type=MESH,
        )

    @pl.loop(1, N)
    def _(k):
        tab_copy(k, me).start()

    tab_all[me] = entry
    tab_all[N] = jnp.full((16, 128), NOBODY, I32)
    xb[BLOCKS - 1, 256:, :] = jnp.zeros((128, 256), BF16)
    sub[:, SUB:, :] = jnp.ones((8, SUB, 1024), BF16)

    @pl.loop(0, BOOKS)
    def _(m):
        words = book_ref[m].astype(F32)
        norm = jnp.sum(words * words, axis=0, keepdims=True)
        first = norm.astype(BF16).astype(F32)
        second = (norm - first).astype(BF16).astype(F32)
        third = norm - first - second
        row = iota((SUB, CODES), 0)
        extra = jnp.where(row == 0, first, jnp.where(row == 1, second, jnp.where(row == 2, third, 0.0)))
        codes[m] = jnp.concatenate([words * -2.0, extra], axis=0).T.astype(BF16)

    r_copy.wait()
    c_copy.wait()

    @pl.loop(0, 4)
    def _(i):
        rows = pl.multiple_of(i * 256, 256)
        for j in range(4):
            rot_t[256 * j : 256 * (j + 1), pl.ds(rows, 256)] = rot[pl.ds(rows, 256), 256 * j : 256 * (j + 1)].T

    @pl.loop(0, 8)
    def _(i):
        rows = pl.multiple_of(i * 256, 256)
        for j in range(4):
            cent_t[256 * j : 256 * (j + 1), pl.ds(rows, 256)] = cent[pl.ds(rows, 256), 256 * j : 256 * (j + 1)].T

    @pl.loop(0, 128)
    def _(t):
        x_copy(t).wait()

    @pl.loop(1, N)
    def _(k):
        tab_copy(k, back(k)).wait_recv()

    lane = iota((16, 128), 1)

    @pl.loop(0, BLOCKS)
    def _(b):
        homes = [tab_all[3 * b + j] + (j << 10) for j in range(3)]
        for s in range(3):
            moved = [pltpu.roll(homes[j], (CAP * (j - s)) % 128, 1) if j != s else homes[j] for j in range(3)]
            found = jnp.where(lane < CAP, moved[0], jnp.where(lane < 2 * CAP, moved[1], moved[2]))
            tab[b, s] = jnp.where(lane < 3 * CAP, found, NOBODY)

    late = jnp.zeros((1, 128), I32)
    first_half = iota((1, 128), 1) < OVER
    for p in range(N // 2):
        left, right = tab_all[2 * p, 11:12, :], tab_all[2 * p + 1, 11:12, :]
        tab_over[p : p + 1, :] = jnp.where(first_half, left, pltpu.roll(right, OVER, 1) + (4 << 8))
        for row in (left, right):
            late = jnp.where(first_half | (((row >> 8) & 63) >= 32), late, 1)
        local_ref[:, 128 * p : 128 * (p + 1)] = tab_over[p : p + 1, :] >> 14
    late = jnp.max(late, axis=1, keepdims=True)
    flag_own[...] = jnp.broadcast_to(late, (8, 128))

    def flag_copy(j, origin):
        return pltpu.make_async_remote_copy(
            src_ref=flag_own,
            dst_ref=flag_all.at[origin],
            send_sem=flag_ss.at[j],
            recv_sem=flag_rs.at[j],
            device_id={"dp": lax.rem(replica + j, DP)},
            device_id_type=MESH,
        )

    for j in range(1, DP):
        flag_copy(j, replica).start()

    def at_owner(b, owner):
        segment = lax.div(owner, 11)
        return tab[b, segment, pl.ds(owner - 11 * segment, 1), :]

    local_ref[:, SLOTS:] = jnp.zeros((1, NEARS * NEAR - SLOTS), I32)
    for b in range(BLOCKS):
        local_ref[:, FIRST + 128 * b : FIRST + 128 * (b + 1)] = at_owner(b, me) >> 14

    mine = pl.ds(pl.multiple_of(core * FS, FS), FS)
    for p in range(N // 2):
        entries = tab_over[p : p + 1, :]
        onehot = onehots(iota((256, 128), 0) == (entries & 255))
        groups = jnp.broadcast_to((entries >> 8) & 63, (FS, 128))
        kept = jnp.zeros((FS, 128), F32)
        for j in range(2):
            home = 2 * p + j
            every = dot(xb[home // 3, 128 * (home % 3) : 128 * (home % 3 + 1), :], onehot)
            for g in range(4):
                kept = jnp.where(groups == 4 * j + g, every[FS * g : FS * (g + 1)], kept)
        wide[p // 8, z, x, mine, 128 * (p % 8) : 128 * (p % 8 + 1)] = kept.astype(BF16)

    def along_x(j):
        return (z * 4 + lax.rem(x + j, 4)) * 2 + core

    def along_z(j):
        return (lax.rem(z + j, 4) * 4 + x) * 2 + core

    def ag_copy(slot, part, device):
        return pltpu.make_async_remote_copy(
            src_ref=part,
            dst_ref=part,
            send_sem=ag_ss.at[slot],
            recv_sem=ag_rs.at[slot],
            device_id={"lists": device},
            device_id_type=MESH,
        )

    def phase(number):
        copies = []
        for half in range(2):
            near_one, far_one = (along_x, along_z) if half == 0 else (along_z, along_x)
            for j in range(1, 4):
                slot = 6 * (number - 1) + 3 * half + j - 1
                if number == 1:
                    copies.append((slot, wide.at[half, z, x, mine, :], near_one(j)))
                elif number == 2 and half == 0:
                    copies.append((slot, wide.at[half, z, :, mine, :], far_one(j)))
                elif number == 2:
                    copies.append((slot, wide.at[half, :, x, mine, :], far_one(j)))
            if number == 3:
                copies.append((12 + half, wide.at[half, :, :, mine, :], me + 1 - 2 * core))
        return copies

    def pieces(number, slot, part):
        if number == 1:
            return [part]
        if number == 2:
            return [part.at[q, :, 512 * h : 512 * (h + 1)] for q in range(4) for h in range(2)]
        return [part.at[q, r] for q in range(4) for r in range(4)]

    def start_phase(number):
        for slot, part, device in phase(number):
            for piece in pieces(number, slot, part):
                ag_copy(slot, piece, device).start()

    def wait_phase(number):
        before = lambda v, j: lax.rem(v + 4 - j, 4)
        theirs = pl.ds(pl.multiple_of((1 - core) * FS, FS), FS)
        for half in range(2):
            for j in range(1, 4):
                slot = 6 * (number - 1) + 3 * half + j - 1
                if number == 1:
                    part = wide.at[half, z, before(x, j), mine, :] if half == 0 else wide.at[half, before(z, j), x, mine, :]
                elif number == 2:
                    part = wide.at[half, before(z, j), :, mine, :] if half == 0 else wide.at[half, :, before(x, j), mine, :]
                else:
                    slot, part = 12 + half, wide.at[half, :, :, theirs, :]
                if number < 3 or j == 1:
                    ag_copy(slot, part, peer(1)).wait_recv()

    start_phase(1)

    def across(i):
        chip = lax.rem(z + lax.rem(i, 4), 4) * 4 + lax.rem(x + lax.rem(lax.div(i, 4) + i, 4), 4)
        return [chip * 2 + core, chip * 2 + 1 - core]

    def vec_copy(part, k, owner, slice_of):
        low, high = PARTS[part]
        return pltpu.make_async_remote_copy(
            src_ref=send.at[k, low:high],
            dst_ref=recv.at[low:high, pl.ds(pl.multiple_of(slice_of * FS, FS), FS), :],
            send_sem=vec_ss.at[part, k],
            recv_sem=vec_rs.at[part, slice_of],
            device_id={"lists": owner},
            device_id_type=MESH,
        )

    def own_copy(part):
        low, high = PARTS[part]
        return pltpu.make_async_copy(
            send.at[0, low:high],
            recv.at[low:high, pl.ds(pl.multiple_of(me * FS, FS), FS), :],
            own_sem.at[part],
        )

    def send_to(part, i):
        owners = across(i)

        @pl.when(i == 0)
        def _():
            own_copy(part).start()

        @pl.when(i > 0)
        def _():
            vec_copy(part, 2 * i, owners[0], me).start()

        vec_copy(part, 2 * i + 1, owners[1], me).start()

    def select_part(part):
        @pl.loop(0, N // GROUP)
        def _(i):
            chips = [GROUP // 2 * i + j for j in range(GROUP // 2)]
            owners = [owner for chip in chips for owner in across(chip)]
            for b in range(*PARTS[part]):
                entries = jnp.concatenate([at_owner(b, owner) for owner in owners], axis=1)
                every = dot(xb[b], onehots(iota((256, 128 * GROUP), 0) == (entries & 255)))
                groups = jnp.broadcast_to((entries >> 8) & 63, (FS, 128 * GROUP))
                kept = jnp.zeros((FS, 128 * GROUP), F32)
                for g in range(12):
                    kept = jnp.where(groups == g, every[FS * g : FS * (g + 1)], kept)
                kept = kept.astype(BF16)
                for j in range(GROUP):
                    send[GROUP * i + j, b] = kept[:, 128 * j : 128 * (j + 1)]

            if part == 0:
                for chip in chips:
                    send_to(part, chip)

                @pl.when(i == EARLY)
                def _():
                    wait_phase(1)
                    start_phase(2)

    for part in range(len(PARTS)):
        select_part(part)

    @pl.loop(0, NEARS)
    def _(t):
        lanes = pl.ds(pl.multiple_of(t * NEAR, 128), NEAR)
        onehot = onehots(iota((LISTS, NEAR), 0) == local_ref[:, lanes])
        near[:, lanes] = dot(cent_t[...], onehot).astype(BF16)

        for part, tile in LATER.items():

            @pl.when(t == tile)
            def _():
                @pl.loop(0, N // 2)
                def _(i):
                    send_to(part, i)

        @pl.when(t == PHASE)
        def _():
            wait_phase(2)
            start_phase(3)

    def encode(width, lanes):
        @pl.loop(0, 2)
        def _(i):
            rows = pl.ds(pl.multiple_of(i * 512, 512), 512)
            turned = dot(rot_t[rows, :], resid[:, :width]).astype(BF16)
            for j in range(8):
                piece = turned[SUB * j : SUB * (j + 1)]
                sub[j, :SUB, :width] = piece
                squares = piece.astype(F32)
                length = jnp.sum(squares * squares, axis=0, keepdims=True)
                least = jnp.min(dot(codes[8 * i + j], sub[j, :, :width]), axis=0, keepdims=True)
                errs[pl.ds(8 * i + j, 1), lanes] = (length + least) * (1.0 / SUB)

    def minus(a, b):
        return (a.astype(F32) - b.astype(F32)).astype(BF16)

    def ret_copy(home, owner):
        return pltpu.make_async_remote_copy(
            src_ref=ret_send.at[home],
            dst_ref=ret_recv.at[owner],
            send_sem=ret_ss.at[home],
            recv_sem=ret_rs.at[owner],
            device_id={"lists": home},
            device_id_type=MESH,
        )

    def overflow():
        wait_phase(3)

        @pl.loop(0, 2)
        def _(half):
            lanes = pl.ds(pl.multiple_of(half * 1024, 1024), 1024)

            @pl.loop(0, 4)
            def _(i):
                for j in range(4):
                    rows = pl.ds(pl.multiple_of(i * 256 + j * 64, 64), 64)
                    resid[rows, :] = minus(wide[half, i, j], near[rows, lanes])

            encode(1024, lanes)

    main_lanes = iota((BOOKS, 128), 1) < 64
    def main(part):
        low, high = PARTS[part]
        own_copy(part).wait()

        @pl.loop(1, N)
        def _(k):
            vec_copy(part, k, peer(1), back(k)).wait_recv()

        width, base = 128 * (high - low), FIRST + 128 * low

        @pl.loop(0, 4)
        def _(i):
            rows = pl.ds(pl.multiple_of(i * 256, 256), 256)
            for b in range(low, high):
                resid[rows, 128 * (b - low) : 128 * (b - low + 1)] = minus(
                    recv[b, rows, :], near[rows, FIRST + 128 * b : FIRST + 128 * (b + 1)]
                )

        encode(width, slice(base, base + width))

    def give_back(part):
        low, high = PARTS[part]
        for home in range(3 * low, min(3 * high, N)):
            least = errs[:, FIRST + 128 * (home // 3) : FIRST + 128 * (home // 3 + 1)]
            if home % 3:
                least = pltpu.roll(least, 128 - CAP * (home % 3), 1)
            more = errs[:, 128 * (home // 2) : 128 * (home // 2 + 1)]
            if home % 2 == 0:
                more = pltpu.roll(more, OVER, 1)
            ret_send[home] = jnp.where(main_lanes, least, more)

        @pl.loop(3 * low, min(3 * high, N))
        def _(home):
            @pl.when(home == me)
            def _():
                ret_recv[home] = ret_send[home]

            @pl.when(home != me)
            def _():
                ret_copy(home, me).start()

    overflow()
    for part in range(len(PARTS)):
        main(part)
        give_back(part)

    for j in range(1, DP):
        flag_copy(j, lax.rem(replica + DP - j, DP)).wait_recv()
        late = jnp.maximum(late, flag_all[lax.rem(replica + DP - j, DP)][:1, :1])
    flag_ref[...] = jnp.broadcast_to(late, (8, 128))

    @pl.loop(1, N)
    def _(k):
        ret_copy(me, peer(k)).wait_recv()

    total = jnp.zeros((2 * BOOKS, HOME), F32)
    for t in range(N // 2):
        got = jnp.concatenate([ret_recv[2 * t], ret_recv[2 * t + 1]], axis=1)
        high = got.astype(BF16)
        low = (got - high.astype(F32)).astype(BF16)
        onehot = onehots(iota((256, HOME), 0) + 256 * t == code_ref[...])
        total = total + dot(jnp.concatenate([high, low], axis=0), onehot)
    out_ref[...] = total[:BOOKS] + total[BOOKS:]

    @pl.loop(1, N)
    def _(k):
        tab_copy(k, me).wait_send()
        ret_copy(peer(k), me).wait_send()
        for part in range(len(PARTS)):
            vec_copy(part, k, peer(1), me).wait_send()

    for number in range(1, 4):
        for copy in phase(number):
            ag_copy(*copy).wait_send()
    for j in range(1, DP):
        flag_copy(j, replica).wait_send()


def fast(embeddings, assign, list_slot, centroids, rotation, codebook):
    vmem = pl.BlockSpec(memory_space=pltpu.VMEM)
    hbm = pl.BlockSpec(memory_space=pl.ANY)
    dma = pltpu.SemaphoreType.DMA
    return pl.pallas_call(
        kernel,
        out_shape=(jax.ShapeDtypeStruct((BOOKS, HOME), F32), jax.ShapeDtypeStruct((8, 128), I32)),
        in_specs=[hbm, vmem, vmem, hbm, hbm, vmem],
        out_specs=(vmem, vmem),
        scratch_shapes=[
            pltpu.VMEM((BLOCKS, 384, 256), BF16),
            pltpu.VMEM((N, BLOCKS, FS, 128), BF16),
            pltpu.VMEM((BLOCKS, D, 128), BF16),
            pltpu.VMEM((2, 4, 4, 2 * FS, 1024), BF16),
            pltpu.VMEM((D, NEARS * NEAR), BF16),
            pltpu.VMEM((LISTS, D), BF16),
            pltpu.VMEM((D, LISTS), BF16),
            pltpu.VMEM((D, D), BF16),
            pltpu.VMEM((D, D), BF16),
            pltpu.VMEM((BOOKS, CODES, 2 * SUB), BF16),
            pltpu.VMEM((16, 128), I32),
            pltpu.VMEM((N + 1, 16, 128), I32),
            pltpu.VMEM((BLOCKS, 3, 16, 128), I32),
            pltpu.VMEM((N // 2, 128), I32),
            pltpu.VMEM((1, NEARS * NEAR), I32),
            pltpu.VMEM((D, 1024), BF16),
            pltpu.VMEM((8, 2 * SUB, 1024), BF16),
            pltpu.VMEM((BOOKS, SLOTS), F32),
            pltpu.VMEM((1, HOME), I32),
            pltpu.VMEM((N, BOOKS, 128), F32),
            pltpu.VMEM((N, BOOKS, 128), F32),
            pltpu.VMEM((8, 128), I32),
            pltpu.VMEM((DP, 8, 128), I32),
            dma((128,)), dma, dma, dma((len(PARTS),)),
            dma((N,)), dma((N,)),
            dma((len(PARTS), N)), dma((len(PARTS), N)),
            dma((N,)), dma((N,)),
            dma((14,)), dma((14,)),
            dma((DP,)), dma((DP,)),
        ],
        compiler_params=pltpu.CompilerParams(
            collective_id=0, has_side_effects=True, vmem_limit_bytes=58 * 2**20
        ),
        name="encode",
    )(
        embeddings.T,
        assign.reshape(1, HOME),
        list_slot.reshape(512, 128),
        centroids,
        rotation.reshape(D, D),
        codebook.transpose(0, 2, 1),
    )


def route_rows(assigned, list_slot, list_width, owner_count):
    slot_index = jnp.take(list_slot, assigned)
    target = slot_index // list_width
    local_row = slot_index - target * list_width
    onehot = (target[..., None] == jnp.arange(owner_count, dtype=jnp.int32)).astype(jnp.int32)
    position = jnp.sum(jnp.cumsum(onehot, axis=-2) * onehot, axis=-1) - 1
    return (target, local_row, position)


def encode_rows(received, row_ids, centroids, rotation, codebook, code_norms):
    senders, slot_count, model_width = received.shape
    flattened = received.reshape(senders * slot_count, model_width)
    centre_rows = jnp.take(centroids, row_ids.reshape(-1), axis=0)
    residual = (flattened.astype(jnp.float32) - centre_rows.astype(jnp.float32)).astype(
        jnp.bfloat16
    )
    rotated = jnp.dot(residual, rotation[0], preferred_element_type=jnp.float32).astype(
        jnp.bfloat16
    )
    book_count, centres, sub_width = codebook.shape

    def one_book(book_index):
        subspace = lax.dynamic_slice_in_dim(rotated, book_index * sub_width, sub_width, 1)
        codewords = lax.dynamic_index_in_dim(codebook, book_index, 0, keepdims=False)
        norm_row = lax.dynamic_index_in_dim(code_norms, book_index, 0, keepdims=False)
        products = lax.dot_general(
            subspace, codewords, (((1,), (1,)), ((), ())), preferred_element_type=jnp.float32
        )
        lengths = jnp.sum(jnp.square(subspace.astype(jnp.float32)), axis=1)
        distance = lengths[:, None] + norm_row[None, :] - 2.0 * products
        return jnp.min(distance, axis=1) / sub_width

    errors = lax.map(one_book, jnp.arange(book_count, dtype=jnp.int32))
    errors = errors.reshape(book_count, senders, slot_count).transpose(1, 0, 2)
    return lax.all_to_all(errors, "lists", split_axis=0, concat_axis=0, tiled=True)


def general(embeddings, assign, list_slot, centroids, rotation, codebook):
    owner_count = lax.axis_size("lists")
    list_width = centroids.shape[0]
    home_rows = assign.shape[0]
    capacity = 3 * home_rows // owner_count
    model_width = rotation.shape[1]
    code_norms = jnp.sum(jnp.square(codebook.astype(jnp.float32)), axis=2)
    target, local_row, position = route_rows(assign, list_slot, list_width, owner_count)
    vectors = lax.all_to_all(embeddings, "lists", split_axis=0, concat_axis=1, tiled=True)
    outgoing = (
        jnp.zeros((owner_count, capacity, model_width), jnp.bfloat16)
        .at[target, position]
        .set(vectors)
    )
    row_ids = jnp.zeros((owner_count, capacity), jnp.int32).at[target, position].set(local_row)
    returned = encode_rows(
        lax.all_to_all(outgoing, "lists", split_axis=0, concat_axis=0, tiled=True),
        lax.all_to_all(row_ids, "lists", split_axis=0, concat_axis=0, tiled=True),
        centroids,
        rotation,
        codebook,
        code_norms,
    )
    return jnp.transpose(returned, (1, 0, 2))[:, target, position]


def shards(*arrays):
    errors, flag = fast(*arrays)
    return lax.cond(flag[0, 0] > 0, lambda: general(*arrays), lambda: errors)


def solution(mesh):
    placed = (
        P("dp", "lists"),
        P(("dp", "lists")),
        P(),
        P("lists", None),
        P("lists", None, None),
        P(),
    )
    return jax.shard_map(
        shards, mesh=mesh, in_specs=placed, out_specs=P(None, ("dp", "lists")), check_vma=False
    )
```

```python
import jax
import jax.numpy as jnp
from jax import lax
from jax.experimental import pallas as pl
from jax.experimental.pallas import tpu as pltpu
from jax.sharding import PartitionSpec as P

MESH = pl.DeviceIdType.MESH
F32 = jnp.float32
BF16 = jnp.bfloat16
I32 = jnp.int32

N = 32
DP = 4
HOME = 1024
D = 1024
FS = 32
LISTS = 2048
BOOKS, CODES, SUB = 16, 256, 64
CAP = 42
OVER = 64
BLOCKS = 11
PARTS = ((0, 4), (4, 8), (8, 11))
FIRST = N * OVER
SLOTS = FIRST + 128 * BLOCKS
NEAR = 512
GROUP = 4
EARLY = 2
PHASE = 2
LATER = {1: 1, 2: 3}
NEARS = -(-SLOTS // NEAR)
NOBODY = 32 << 8


def dot(a, b):
    return jnp.dot(a, b, preferred_element_type=F32)


def iota(shape, dim):
    return lax.broadcasted_iota(I32, shape, dim)


def onehots(mask):
    return mask.astype(F32).astype(BF16)


def routes(assign_ref, slots_ref):
    assigned = assign_ref[...]
    table = slots_ref[...].astype(F32).T.astype(I32)
    table = jnp.concatenate([table >> 8, table & 255], axis=0).astype(F32).astype(BF16)
    picked = dot(table, onehots(iota((512, HOME), 0) == (assigned >> 7)))
    low = iota((128, HOME), 0) == (assigned & 127)
    upper = jnp.sum(jnp.where(low, picked[:128], 0.0), axis=0, keepdims=True)
    lower = jnp.sum(jnp.where(low, picked[128:], 0.0), axis=0, keepdims=True)
    slot = upper.astype(I32) * 256 + lower.astype(I32)
    target, local = slot >> 11, slot & (LISTS - 1)
    mine = iota((N, HOME), 0) == target
    before = onehots(iota((HOME, HOME), 0) < iota((HOME, HOME), 1))
    ahead = dot(onehots(mine), before)
    rank = jnp.sum(jnp.where(mine, ahead, 0.0), axis=0, keepdims=True).astype(I32)
    over = rank >= CAP
    over_rank = dot(jnp.broadcast_to(onehots(over), (8, HOME)), before)[:1].astype(I32)
    segment = (target >= 11).astype(I32) + (target >= 22).astype(I32)
    row = jnp.where(over, 11, target - 11 * segment)
    lane = jnp.where(over, over_rank, CAP * segment + rank)
    mine = iota((16, HOME), 0) == row
    place = onehots(iota((128, HOME), 0) == lane)
    vector = iota((1, HOME), 1)
    fields = [vector & 255, vector >> 8, local & 255, local >> 8, jnp.ones_like(vector)]
    planes = [jnp.where(mine, field.astype(F32), 0.0) for field in fields]
    planes = jnp.concatenate(planes, axis=0).astype(BF16)
    held = lax.dot_general(planes, place, (((1,), (1,)), ((), ())), preferred_element_type=F32).astype(I32)
    index, group, local_low, local_high, valid = (held[16 * j : 16 * (j + 1)] for j in range(5))
    entry = index + (group << 8) + (local_low << 14) + (local_high << 22)
    entry = jnp.where(valid > 0, entry, NOBODY)
    return target * 128 + jnp.where(over, 64 + over_rank, rank), entry


def kernel(
    emb_ref, assign_ref, slots_ref, cent_ref, rot_ref, book_ref, out_ref, flag_ref,
    xb, send, recv, wide, near, cent, cent_t, rot, rot_t, codes, tab_own, tab_all, tab, tab_over, local_ref,
    resid, sub, errs, code_ref, ret_send, ret_recv, flag_own, flag_all,
    x_sem, c_sem, r_sem, own_sem, tab_ss, tab_rs, vec_ss, vec_rs, ret_ss, ret_rs, ag_ss, ag_rs, flag_ss, flag_rs,
):
    me = lax.axis_index("lists")
    replica = lax.axis_index("dp")
    core = lax.rem(me, 2)
    x = lax.rem(lax.div(me, 2), 4)
    z = lax.div(me, 8)

    def peer(k):
        return lax.rem(me + k, N)

    def all_of(ref, send_sem, recv_sem):
        return pltpu.make_async_remote_copy(
            src_ref=ref, dst_ref=ref, send_sem=send_sem, recv_sem=recv_sem,
            device_id={"lists": peer(1)}, device_id_type=MESH,
        )

    def all_tables():
        return all_of(tab_all.at[: N - 1], tab_ss, tab_rs)

    def all_vectors(part):
        low, high = PARTS[part]
        return all_of(send.at[1:, low:high], vec_ss.at[part], vec_rs.at[part])

    def all_returns():
        return all_of(ret_recv.at[: N - 1], ret_ss, ret_rs)

    barrier = pltpu.get_barrier_semaphore()

    @pl.loop(1, N)
    def _(k):
        pl.semaphore_signal(barrier, inc=1, device_id={"lists": peer(k)}, device_id_type=MESH)

    for j in range(1, DP):
        other = lax.rem(replica + j, DP)
        pl.semaphore_signal(barrier, inc=1, device_id={"dp": other}, device_id_type=MESH)

    def x_copy(t):
        block = lax.div(t, 12)
        group = t - block * 12
        return pltpu.make_async_copy(
            emb_ref.at[:, pl.ds(pl.multiple_of(t * 256, 256), 256)],
            xb.at[block, pl.ds(pl.multiple_of(group * FS, FS), FS), :],
            x_sem.at[lax.div(t, 120)],
        )

    c_copy = pltpu.make_async_copy(cent_ref, cent, c_sem)
    r_copy = pltpu.make_async_copy(rot_ref, rot, r_sem)
    c_copy.start()
    r_copy.start()

    code, entry = routes(assign_ref, slots_ref)
    code_ref[...] = code
    tab_own[...] = entry

    pl.semaphore_wait(barrier, N - 1 + DP - 1)

    def tab_copy(k, home):
        return pltpu.make_async_remote_copy(
            src_ref=tab_own,
            dst_ref=tab_all.at[home],
            send_sem=tab_ss,
            recv_sem=tab_rs,
            device_id={"lists": peer(k)},
            device_id_type=MESH,
        )

    @pl.loop(1, N)
    def _(k):
        tab_copy(k, me).start()

    @pl.loop(0, 128)
    def _(t):
        x_copy(t).start()

    tab_all[me] = entry
    tab_all[N] = jnp.full((16, 128), NOBODY, I32)
    xb[BLOCKS - 1, 256:, :] = jnp.zeros((128, 256), BF16)
    sub[:, SUB:, :] = jnp.ones((8, SUB, 1024), BF16)

    @pl.loop(0, BOOKS)
    def _(m):
        words = book_ref[m].astype(F32)
        norm = jnp.sum(words * words, axis=0, keepdims=True)
        first = norm.astype(BF16).astype(F32)
        second = (norm - first).astype(BF16).astype(F32)
        third = norm - first - second
        row = iota((SUB, CODES), 0)
        extra = jnp.where(row == 0, first, jnp.where(row == 1, second, jnp.where(row == 2, third, 0.0)))
        codes[m] = jnp.concatenate([words * -2.0, extra], axis=0).T.astype(BF16)

    r_copy.wait()
    c_copy.wait()

    @pl.loop(0, 4)
    def _(i):
        rows = pl.multiple_of(i * 256, 256)
        for j in range(4):
            rot_t[256 * j : 256 * (j + 1), pl.ds(rows, 256)] = rot[pl.ds(rows, 256), 256 * j : 256 * (j + 1)].T

    @pl.loop(0, 8)
    def _(i):
        rows = pl.multiple_of(i * 256, 256)
        for j in range(4):
            cent_t[256 * j : 256 * (j + 1), pl.ds(rows, 256)] = cent[pl.ds(rows, 256), 256 * j : 256 * (j + 1)].T

    pltpu.make_async_copy(xb.at[:10], xb.at[:10], x_sem.at[0]).wait()
    pltpu.make_async_copy(xb.at[10, :256], xb.at[10, :256], x_sem.at[1]).wait()

    all_tables().wait_recv()

    lane = iota((16, 128), 1)

    @pl.loop(0, BLOCKS)
    def _(b):
        homes = [tab_all[3 * b + j] + (j << 10) for j in range(3)]
        for s in range(3):
            moved = [pltpu.roll(homes[j], (CAP * (j - s)) % 128, 1) if j != s else homes[j] for j in range(3)]
            found = jnp.where(lane < CAP, moved[0], jnp.where(lane < 2 * CAP, moved[1], moved[2]))
            tab[b, s] = jnp.where(lane < 3 * CAP, found, NOBODY)

    late = jnp.zeros((1, 128), I32)
    first_half = iota((1, 128), 1) < OVER
    for p in range(N // 2):
        left, right = tab_all[2 * p, 11:12, :], tab_all[2 * p + 1, 11:12, :]
        tab_over[p : p + 1, :] = jnp.where(first_half, left, pltpu.roll(right, OVER, 1) + (4 << 8))
        for row in (left, right):
            late = jnp.where(first_half | (((row >> 8) & 63) >= 32), late, 1)
        local_ref[:, 128 * p : 128 * (p + 1)] = tab_over[p : p + 1, :] >> 14
    late = jnp.max(late, axis=1, keepdims=True)
    flag_own[...] = jnp.broadcast_to(late, (8, 128))

    def flag_copy(j, origin):
        return pltpu.make_async_remote_copy(
            src_ref=flag_own,
            dst_ref=flag_all.at[origin],
            send_sem=flag_ss.at[j],
            recv_sem=flag_rs.at[j],
            device_id={"dp": lax.rem(replica + j, DP)},
            device_id_type=MESH,
        )

    for j in range(1, DP):
        flag_copy(j, replica).start()

    def at_owner(b, owner):
        segment = lax.div(owner, 11)
        return tab[b, segment, pl.ds(owner - 11 * segment, 1), :]

    local_ref[:, SLOTS:] = jnp.zeros((1, NEARS * NEAR - SLOTS), I32)
    for b in range(BLOCKS):
        local_ref[:, FIRST + 128 * b : FIRST + 128 * (b + 1)] = at_owner(b, me) >> 14

    mine = pl.ds(pl.multiple_of(core * FS, FS), FS)
    for p in range(N // 2):
        entries = tab_over[p : p + 1, :]
        onehot = onehots(iota((256, 128), 0) == (entries & 255))
        groups = jnp.broadcast_to((entries >> 8) & 63, (FS, 128))
        kept = jnp.zeros((FS, 128), F32)
        for j in range(2):
            home = 2 * p + j
            every = dot(xb[home // 3, 128 * (home % 3) : 128 * (home % 3 + 1), :], onehot)
            for g in range(4):
                kept = jnp.where(groups == 4 * j + g, every[FS * g : FS * (g + 1)], kept)
        wide[p // 8, z, x, mine, 128 * (p % 8) : 128 * (p % 8 + 1)] = kept.astype(BF16)

    def along_x(j):
        return (z * 4 + lax.rem(x + j, 4)) * 2 + core

    def along_z(j):
        return (lax.rem(z + j, 4) * 4 + x) * 2 + core

    def ag_copy(slot, part, device):
        return pltpu.make_async_remote_copy(
            src_ref=part,
            dst_ref=part,
            send_sem=ag_ss.at[slot],
            recv_sem=ag_rs.at[slot],
            device_id={"lists": device},
            device_id_type=MESH,
        )

    def phase(number):
        copies = []
        for half in range(2):
            near_one, far_one = (along_x, along_z) if half == 0 else (along_z, along_x)
            for j in range(1, 4):
                slot = 6 * (number - 1) + 3 * half + j - 1
                if number == 1:
                    copies.append((slot, wide.at[half, z, x, mine, :], near_one(j)))
                elif number == 2 and half == 0:
                    copies.append((slot, wide.at[half, z, :, mine, :], far_one(j)))
                elif number == 2:
                    copies.append((slot, wide.at[half, :, x, mine, :], far_one(j)))
            if number == 3:
                copies.append((12 + half, wide.at[half, :, :, mine, :], me + 1 - 2 * core))
        return copies

    def pieces(number, slot, part):
        if number == 1:
            return [part]
        if number == 2:
            return [part.at[q] for q in range(4)]
        return [part.at[q] for q in range(4)]

    def start_phase(number):
        for slot, part, device in phase(number):
            for piece in pieces(number, slot, part):
                ag_copy(slot, piece, device).start()

    def wait_phase(number):
        before = lambda v, j: lax.rem(v + 4 - j, 4)
        theirs = pl.ds(pl.multiple_of((1 - core) * FS, FS), FS)
        for half in range(2):
            for j in range(1, 4):
                slot = 6 * (number - 1) + 3 * half + j - 1
                if number == 1:
                    part = wide.at[half, z, before(x, j), mine, :] if half == 0 else wide.at[half, before(z, j), x, mine, :]
                elif number == 2:
                    part = wide.at[half, before(z, j), :, mine, :] if half == 0 else wide.at[half, :, before(x, j), mine, :]
                else:
                    slot, part = 12 + half, wide.at[half, :, :, theirs, :]
                if number < 3 or j == 1:
                    ag_copy(slot, part, peer(1)).wait_recv()

    start_phase(1)

    def across(i):
        chip = lax.rem(z + lax.rem(i, 4), 4) * 4 + lax.rem(x + lax.rem(lax.div(i, 4) + i, 4), 4)
        return [chip * 2 + core, chip * 2 + 1 - core]

    def vec_copy(part, k, owner, slice_of):
        low, high = PARTS[part]
        return pltpu.make_async_remote_copy(
            src_ref=send.at[k, low:high],
            dst_ref=recv.at[low:high, pl.ds(pl.multiple_of(slice_of * FS, FS), FS), :],
            send_sem=vec_ss.at[part],
            recv_sem=vec_rs.at[part],
            device_id={"lists": owner},
            device_id_type=MESH,
        )

    def own_copy(part):
        low, high = PARTS[part]
        return pltpu.make_async_copy(
            send.at[0, low:high],
            recv.at[low:high, pl.ds(pl.multiple_of(me * FS, FS), FS), :],
            own_sem.at[part],
        )

    def send_to(part, i):
        owners = across(i)

        @pl.when(i == 0)
        def _():
            own_copy(part).start()

        @pl.when(i > 0)
        def _():
            vec_copy(part, 2 * i, owners[0], me).start()

        vec_copy(part, 2 * i + 1, owners[1], me).start()

    def select_part(part):
        @pl.loop(0, N // GROUP)
        def _(i):
            chips = [GROUP // 2 * i + j for j in range(GROUP // 2)]
            owners = [owner for chip in chips for owner in across(chip)]
            for b in range(*PARTS[part]):
                entries = jnp.concatenate([at_owner(b, owner) for owner in owners], axis=1)
                every = dot(xb[b], onehots(iota((256, 128 * GROUP), 0) == (entries & 255)))
                groups = jnp.broadcast_to((entries >> 8) & 63, (FS, 128 * GROUP))
                kept = jnp.zeros((FS, 128 * GROUP), F32)
                for g in range(12):
                    kept = jnp.where(groups == g, every[FS * g : FS * (g + 1)], kept)
                kept = kept.astype(BF16)
                for j in range(GROUP):
                    send[GROUP * i + j, b] = kept[:, 128 * j : 128 * (j + 1)]

            if part == 0:
                for chip in chips:
                    send_to(part, chip)

                @pl.when(i == EARLY)
                def _():
                    wait_phase(1)
                    start_phase(2)

    for part in range(len(PARTS)):
        select_part(part)

    @pl.loop(0, NEARS)
    def _(t):
        lanes = pl.ds(pl.multiple_of(t * NEAR, 128), NEAR)
        onehot = onehots(iota((LISTS, NEAR), 0) == local_ref[:, lanes])
        near[:, lanes] = dot(cent_t[...], onehot).astype(BF16)

        for part, tile in LATER.items():

            @pl.when(t == tile)
            def _():
                @pl.loop(0, N // 2)
                def _(i):
                    send_to(part, i)

        @pl.when(t == PHASE)
        def _():
            wait_phase(2)
            start_phase(3)

    def encode(width, lanes):
        @pl.loop(0, 2)
        def _(i):
            rows = pl.ds(pl.multiple_of(i * 512, 512), 512)
            turned = dot(rot_t[rows, :], resid[:, :width]).astype(BF16)
            for j in range(8):
                piece = turned[SUB * j : SUB * (j + 1)]
                sub[j, :SUB, :width] = piece
                squares = piece.astype(F32)
                length = jnp.sum(squares * squares, axis=0, keepdims=True)
                least = jnp.min(dot(codes[8 * i + j], sub[j, :, :width]), axis=0, keepdims=True)
                errs[pl.ds(8 * i + j, 1), lanes] = (length + least) * (1.0 / SUB)

    def minus(a, b):
        return (a.astype(F32) - b.astype(F32)).astype(BF16)

    def ret_copy(home, owner):
        return pltpu.make_async_remote_copy(
            src_ref=ret_send.at[home],
            dst_ref=ret_recv.at[owner],
            send_sem=ret_ss,
            recv_sem=ret_rs,
            device_id={"lists": home},
            device_id_type=MESH,
        )

    def overflow():
        wait_phase(3)

        @pl.loop(0, 2)
        def _(half):
            lanes = pl.ds(pl.multiple_of(half * 1024, 1024), 1024)

            @pl.loop(0, 4)
            def _(i):
                for j in range(4):
                    rows = pl.ds(pl.multiple_of(i * 256 + j * 64, 64), 64)
                    resid[rows, :] = minus(wide[half, i, j], near[rows, lanes])

            encode(1024, lanes)

    main_lanes = iota((BOOKS, 128), 1) < 64
    def main(part):
        low, high = PARTS[part]
        own_copy(part).wait()

        all_vectors(part).wait_recv()

        width, base = 128 * (high - low), FIRST + 128 * low

        @pl.loop(0, 4)
        def _(i):
            rows = pl.ds(pl.multiple_of(i * 256, 256), 256)
            for b in range(low, high):
                resid[rows, 128 * (b - low) : 128 * (b - low + 1)] = minus(
                    recv[b, rows, :], near[rows, FIRST + 128 * b : FIRST + 128 * (b + 1)]
                )

        encode(width, slice(base, base + width))

    def give_back(part):
        low, high = PARTS[part]
        for home in range(3 * low, min(3 * high, N)):
            least = errs[:, FIRST + 128 * (home // 3) : FIRST + 128 * (home // 3 + 1)]
            if home % 3:
                least = pltpu.roll(least, 128 - CAP * (home % 3), 1)
            more = errs[:, 128 * (home // 2) : 128 * (home // 2 + 1)]
            if home % 2 == 0:
                more = pltpu.roll(more, OVER, 1)
            ret_send[home] = jnp.where(main_lanes, least, more)

        @pl.loop(3 * low, min(3 * high, N))
        def _(home):
            @pl.when(home == me)
            def _():
                ret_recv[home] = ret_send[home]

            @pl.when(home != me)
            def _():
                ret_copy(home, me).start()

    overflow()
    for part in range(len(PARTS)):
        main(part)
        give_back(part)

    for j in range(1, DP):
        flag_copy(j, lax.rem(replica + DP - j, DP)).wait_recv()
        late = jnp.maximum(late, flag_all[lax.rem(replica + DP - j, DP)][:1, :1])
    flag_ref[...] = jnp.broadcast_to(late, (8, 128))

    all_tables().wait_send()
    for part in range(len(PARTS)):
        all_vectors(part).wait_send()
    for number in range(1, 4):
        for copy in phase(number):
            ag_copy(*copy).wait_send()
    for j in range(1, DP):
        flag_copy(j, replica).wait_send()

    all_returns().wait_recv()

    total = jnp.zeros((2 * BOOKS, HOME), F32)
    for t in range(N // 2):
        got = jnp.concatenate([ret_recv[2 * t], ret_recv[2 * t + 1]], axis=1)
        high = got.astype(BF16)
        low = (got - high.astype(F32)).astype(BF16)
        onehot = onehots(iota((256, HOME), 0) + 256 * t == code_ref[...])
        total = total + dot(jnp.concatenate([high, low], axis=0), onehot)
    out_ref[...] = total[:BOOKS] + total[BOOKS:]

    all_returns().wait_send()


def fast(embeddings, assign, list_slot, centroids, rotation, codebook):
    vmem = pl.BlockSpec(memory_space=pltpu.VMEM)
    hbm = pl.BlockSpec(memory_space=pl.ANY)
    dma = pltpu.SemaphoreType.DMA
    return pl.pallas_call(
        kernel,
        out_shape=(jax.ShapeDtypeStruct((BOOKS, HOME), F32), jax.ShapeDtypeStruct((8, 128), I32)),
        in_specs=[hbm, vmem, vmem, hbm, hbm, vmem],
        out_specs=(vmem, vmem),
        scratch_shapes=[
            pltpu.VMEM((BLOCKS, 384, 256), BF16),
            pltpu.VMEM((N, BLOCKS, FS, 128), BF16),
            pltpu.VMEM((BLOCKS, D, 128), BF16),
            pltpu.VMEM((2, 4, 4, 2 * FS, 1024), BF16),
            pltpu.VMEM((D, NEARS * NEAR), BF16),
            pltpu.VMEM((LISTS, D), BF16),
            pltpu.VMEM((D, LISTS), BF16),
            pltpu.VMEM((D, D), BF16),
            pltpu.VMEM((D, D), BF16),
            pltpu.VMEM((BOOKS, CODES, 2 * SUB), BF16),
            pltpu.VMEM((16, 128), I32),
            pltpu.VMEM((N + 1, 16, 128), I32),
            pltpu.VMEM((BLOCKS, 3, 16, 128), I32),
            pltpu.VMEM((N // 2, 128), I32),
            pltpu.VMEM((1, NEARS * NEAR), I32),
            pltpu.VMEM((D, 1024), BF16),
            pltpu.VMEM((8, 2 * SUB, 1024), BF16),
            pltpu.VMEM((BOOKS, SLOTS), F32),
            pltpu.VMEM((1, HOME), I32),
            pltpu.VMEM((N, BOOKS, 128), F32),
            pltpu.VMEM((N, BOOKS, 128), F32),
            pltpu.VMEM((8, 128), I32),
            pltpu.VMEM((DP, 8, 128), I32),
            dma((2,)), dma, dma, dma((len(PARTS),)),
            dma, dma,
            dma((len(PARTS),)), dma((len(PARTS),)),
            dma, dma,
            dma((14,)), dma((14,)),
            dma((DP,)), dma((DP,)),
        ],
        compiler_params=pltpu.CompilerParams(
            collective_id=0, has_side_effects=True, vmem_limit_bytes=58 * 2**20
        ),
        name="encode",
    )(
        embeddings.T,
        assign.reshape(1, HOME),
        list_slot.reshape(512, 128),
        centroids,
        rotation.reshape(D, D),
        codebook.transpose(0, 2, 1),
    )


def route_rows(assigned, list_slot, list_width, owner_count):
    slot_index = jnp.take(list_slot, assigned)
    target = slot_index // list_width
    local_row = slot_index - target * list_width
    onehot = (target[..., None] == jnp.arange(owner_count, dtype=jnp.int32)).astype(jnp.int32)
    position = jnp.sum(jnp.cumsum(onehot, axis=-2) * onehot, axis=-1) - 1
    return (target, local_row, position)


def encode_rows(received, row_ids, centroids, rotation, codebook, code_norms):
    senders, slot_count, model_width = received.shape
    flattened = received.reshape(senders * slot_count, model_width)
    centre_rows = jnp.take(centroids, row_ids.reshape(-1), axis=0)
    residual = (flattened.astype(jnp.float32) - centre_rows.astype(jnp.float32)).astype(
        jnp.bfloat16
    )
    rotated = jnp.dot(residual, rotation[0], preferred_element_type=jnp.float32).astype(
        jnp.bfloat16
    )
    book_count, centres, sub_width = codebook.shape

    def one_book(book_index):
        subspace = lax.dynamic_slice_in_dim(rotated, book_index * sub_width, sub_width, 1)
        codewords = lax.dynamic_index_in_dim(codebook, book_index, 0, keepdims=False)
        norm_row = lax.dynamic_index_in_dim(code_norms, book_index, 0, keepdims=False)
        products = lax.dot_general(
            subspace, codewords, (((1,), (1,)), ((), ())), preferred_element_type=jnp.float32
        )
        lengths = jnp.sum(jnp.square(subspace.astype(jnp.float32)), axis=1)
        distance = lengths[:, None] + norm_row[None, :] - 2.0 * products
        return jnp.min(distance, axis=1) / sub_width

    errors = lax.map(one_book, jnp.arange(book_count, dtype=jnp.int32))
    errors = errors.reshape(book_count, senders, slot_count).transpose(1, 0, 2)
    return lax.all_to_all(errors, "lists", split_axis=0, concat_axis=0, tiled=True)


def general(embeddings, assign, list_slot, centroids, rotation, codebook):
    owner_count = lax.axis_size("lists")
    list_width = centroids.shape[0]
    home_rows = assign.shape[0]
    capacity = 3 * home_rows // owner_count
    model_width = rotation.shape[1]
    code_norms = jnp.sum(jnp.square(codebook.astype(jnp.float32)), axis=2)
    target, local_row, position = route_rows(assign, list_slot, list_width, owner_count)
    vectors = lax.all_to_all(embeddings, "lists", split_axis=0, concat_axis=1, tiled=True)
    outgoing = (
        jnp.zeros((owner_count, capacity, model_width), jnp.bfloat16)
        .at[target, position]
        .set(vectors)
    )
    row_ids = jnp.zeros((owner_count, capacity), jnp.int32).at[target, position].set(local_row)
    returned = encode_rows(
        lax.all_to_all(outgoing, "lists", split_axis=0, concat_axis=0, tiled=True),
        lax.all_to_all(row_ids, "lists", split_axis=0, concat_axis=0, tiled=True),
        centroids,
        rotation,
        codebook,
        code_norms,
    )
    return jnp.transpose(returned, (1, 0, 2))[:, target, position]


def shards(*arrays):
    errors, flag = fast(*arrays)
    return lax.cond(flag[0, 0] > 0, lambda: general(*arrays), lambda: errors)


def solution(mesh):
    placed = (
        P("dp", "lists"),
        P(("dp", "lists")),
        P(),
        P("lists", None),
        P("lists", None, None),
        P(),
    )
    return jax.shard_map(
        shards, mesh=mesh, in_specs=placed, out_specs=P(None, ("dp", "lists")), check_vma=False
    )
```

```python
import jax
import jax.numpy as jnp
from jax import lax
from jax.experimental import pallas as pl
from jax.experimental.pallas import tpu as pltpu
from jax.sharding import PartitionSpec as P

MESH = pl.DeviceIdType.MESH
F32 = jnp.float32
BF16 = jnp.bfloat16
I32 = jnp.int32

N = 32
DP = 4
HOME = 1024
D = 1024
FS = 32
LISTS = 2048
BOOKS, CODES, SUB = 16, 256, 64
CAP = 42
OVER = 64
BLOCKS = 11
PARTS = ((0, 4), (4, 8), (8, 11))
FIRST = N * OVER
SLOTS = FIRST + 128 * BLOCKS
NEAR = 512
GROUP = 8
EARLY = 1
PHASE = 2
LATER = {1: 1, 2: 3}
NEARS = -(-SLOTS // NEAR)
NOBODY = 32 << 8


def dot(a, b):
    return jnp.dot(a, b, preferred_element_type=F32)


def iota(shape, dim):
    return lax.broadcasted_iota(I32, shape, dim)


def onehots(mask):
    return mask.astype(F32).astype(BF16)


def routes(assign_ref, slots_ref):
    assigned = assign_ref[...]
    table = slots_ref[...].astype(F32).T.astype(I32)
    table = jnp.concatenate([table >> 8, table & 255], axis=0).astype(F32).astype(BF16)
    picked = dot(table, onehots(iota((512, HOME), 0) == (assigned >> 7)))
    low = iota((128, HOME), 0) == (assigned & 127)
    upper = jnp.sum(jnp.where(low, picked[:128], 0.0), axis=0, keepdims=True)
    lower = jnp.sum(jnp.where(low, picked[128:], 0.0), axis=0, keepdims=True)
    slot = upper.astype(I32) * 256 + lower.astype(I32)
    target, local = slot >> 11, slot & (LISTS - 1)
    mine = iota((N, HOME), 0) == target
    before = onehots(iota((HOME, HOME), 0) < iota((HOME, HOME), 1))
    ahead = dot(onehots(mine), before)
    rank = jnp.sum(jnp.where(mine, ahead, 0.0), axis=0, keepdims=True).astype(I32)
    over = rank >= CAP
    over_rank = dot(jnp.broadcast_to(onehots(over), (8, HOME)), before)[:1].astype(I32)
    segment = (target >= 11).astype(I32) + (target >= 22).astype(I32)
    row = jnp.where(over, 11, target - 11 * segment)
    lane = jnp.where(over, over_rank, CAP * segment + rank)
    mine = iota((16, HOME), 0) == row
    place = onehots(iota((128, HOME), 0) == lane)
    vector = iota((1, HOME), 1)
    fields = [vector & 255, vector >> 8, local & 255, local >> 8, jnp.ones_like(vector)]
    planes = [jnp.where(mine, field.astype(F32), 0.0) for field in fields]
    planes = jnp.concatenate(planes, axis=0).astype(BF16)
    held = lax.dot_general(planes, place, (((1,), (1,)), ((), ())), preferred_element_type=F32).astype(I32)
    index, group, local_low, local_high, valid = (held[16 * j : 16 * (j + 1)] for j in range(5))
    entry = index + (group << 8) + (local_low << 14) + (local_high << 22)
    entry = jnp.where(valid > 0, entry, NOBODY)
    return target * 128 + jnp.where(over, 64 + over_rank, rank), entry


def kernel(
    emb_ref, assign_ref, slots_ref, cent_ref, rot_ref, book_ref, out_ref, flag_ref,
    xb, send, recv, wide, near, cent, cent_t, rot, rot_t, codes, tab_own, tab_all, tab, tab_over, local_ref,
    resid, sub, errs, code_ref, ret_send, ret_recv, arrive, flag_own, flag_all,
    x_sem, c_sem, r_sem, own_sem, tab_ss, tab_rs, vec_ss, vec_rs, ret_ss, ret_rs, ag_ss, ag_rs, flag_ss, flag_rs,
):
    me = lax.axis_index("lists")
    replica = lax.axis_index("dp")
    core = lax.rem(me, 2)
    x = lax.rem(lax.div(me, 2), 4)
    z = lax.div(me, 8)

    def peer(k):
        return lax.rem(me + k, N)

    def all_of(ref, send_sem, recv_sem):
        return pltpu.make_async_remote_copy(
            src_ref=ref, dst_ref=ref, send_sem=send_sem, recv_sem=recv_sem,
            device_id={"lists": peer(1)}, device_id_type=MESH,
        )

    def all_tables():
        return all_of(tab_all.at[: N - 1], tab_ss, tab_rs)

    def all_vectors(part):
        low, high = PARTS[part]
        return all_of(send.at[1:, low:high], vec_ss.at[part], vec_rs.at[part])

    def all_returns():
        return all_of(ret_recv.at[: N - 1], ret_ss, ret_rs)

    barrier = pltpu.get_barrier_semaphore()

    @pl.loop(1, N)
    def _(k):
        pl.semaphore_signal(barrier, inc=1, device_id={"lists": peer(k)}, device_id_type=MESH)

    for j in range(1, DP):
        other = lax.rem(replica + j, DP)
        pl.semaphore_signal(barrier, inc=1, device_id={"dp": other}, device_id_type=MESH)

    def x_copy(t):
        block = lax.div(t, 12)
        group = t - block * 12
        return pltpu.make_async_copy(
            emb_ref.at[:, pl.ds(pl.multiple_of(t * 256, 256), 256)],
            xb.at[block, pl.ds(pl.multiple_of(group * FS, FS), FS), :],
            x_sem.at[lax.div(t, 120)],
        )

    c_copy = pltpu.make_async_copy(cent_ref, cent, c_sem)
    r_copy = pltpu.make_async_copy(rot_ref, rot, r_sem)
    c_copy.start()
    r_copy.start()

    code, entry = routes(assign_ref, slots_ref)
    code_ref[...] = code
    tab_own[...] = entry

    pl.semaphore_wait(barrier, N - 1 + DP - 1)

    def tab_copy(k, home):
        return pltpu.make_async_remote_copy(
            src_ref=tab_own,
            dst_ref=tab_all.at[home],
            send_sem=tab_ss,
            recv_sem=tab_rs,
            device_id={"lists": peer(k)},
            device_id_type=MESH,
        )

    @pl.loop(1, N)
    def _(k):
        tab_copy(k, me).start()

    @pl.loop(0, 128)
    def _(t):
        x_copy(t).start()

    tab_all[me] = entry
    tab_all[N] = jnp.full((16, 128), NOBODY, I32)
    xb[BLOCKS - 1, 256:, :] = jnp.zeros((128, 256), BF16)
    sub[:, SUB:, :] = jnp.ones((16, SUB, 1024), BF16)

    @pl.loop(0, BOOKS)
    def _(m):
        words = book_ref[m].astype(F32)
        norm = jnp.sum(words * words, axis=0, keepdims=True)
        first = norm.astype(BF16).astype(F32)
        second = (norm - first).astype(BF16).astype(F32)
        third = norm - first - second
        row = iota((SUB, CODES), 0)
        extra = jnp.where(row == 0, first, jnp.where(row == 1, second, jnp.where(row == 2, third, 0.0)))
        codes[m] = jnp.concatenate([words * -2.0, extra], axis=0).T.astype(BF16)

    r_copy.wait()
    c_copy.wait()

    @pl.loop(0, 4)
    def _(i):
        rows = pl.multiple_of(i * 256, 256)
        for j in range(4):
            rot_t[256 * j : 256 * (j + 1), pl.ds(rows, 256)] = rot[pl.ds(rows, 256), 256 * j : 256 * (j + 1)].T

    @pl.loop(0, 8)
    def _(i):
        rows = pl.multiple_of(i * 256, 256)
        for j in range(4):
            cent_t[256 * j : 256 * (j + 1), pl.ds(rows, 256)] = cent[pl.ds(rows, 256), 256 * j : 256 * (j + 1)].T

    pltpu.make_async_copy(xb.at[:10], xb.at[:10], x_sem.at[0]).wait()
    pltpu.make_async_copy(xb.at[10, :256], xb.at[10, :256], x_sem.at[1]).wait()

    all_tables().wait_recv()

    lane = iota((16, 128), 1)

    @pl.loop(0, BLOCKS)
    def _(b):
        homes = [tab_all[3 * b + j] + (j << 10) for j in range(3)]
        for s in range(3):
            moved = [pltpu.roll(homes[j], (CAP * (j - s)) % 128, 1) if j != s else homes[j] for j in range(3)]
            found = jnp.where(lane < CAP, moved[0], jnp.where(lane < 2 * CAP, moved[1], moved[2]))
            tab[b, s] = jnp.where(lane < 3 * CAP, found, NOBODY)

    late = jnp.zeros((1, 128), I32)
    first_half = iota((1, 128), 1) < OVER
    for p in range(N // 2):
        left, right = tab_all[2 * p, 11:12, :], tab_all[2 * p + 1, 11:12, :]
        tab_over[p : p + 1, :] = jnp.where(first_half, left, pltpu.roll(right, OVER, 1) + (4 << 8))
        for row in (left, right):
            late = jnp.where(first_half | (((row >> 8) & 63) >= 32), late, 1)
        local_ref[:, 128 * p : 128 * (p + 1)] = tab_over[p : p + 1, :] >> 14
    late = jnp.max(late, axis=1, keepdims=True)
    flag_own[...] = jnp.broadcast_to(late, (8, 128))

    def flag_copy(j, origin):
        return pltpu.make_async_remote_copy(
            src_ref=flag_own,
            dst_ref=flag_all.at[origin],
            send_sem=flag_ss.at[j],
            recv_sem=flag_rs.at[j],
            device_id={"dp": lax.rem(replica + j, DP)},
            device_id_type=MESH,
        )

    for j in range(1, DP):
        flag_copy(j, replica).start()

    def at_owner(b, owner):
        segment = lax.div(owner, 11)
        return tab[b, segment, pl.ds(owner - 11 * segment, 1), :]

    local_ref[:, SLOTS:] = jnp.zeros((1, NEARS * NEAR - SLOTS), I32)
    for b in range(BLOCKS):
        local_ref[:, FIRST + 128 * b : FIRST + 128 * (b + 1)] = at_owner(b, me) >> 14

    mine = pl.ds(pl.multiple_of(core * FS, FS), FS)
    for p in range(N // 2):
        entries = tab_over[p : p + 1, :]
        onehot = onehots(iota((256, 128), 0) == (entries & 255))
        groups = jnp.broadcast_to((entries >> 8) & 63, (FS, 128))
        kept = jnp.zeros((FS, 128), F32)
        for j in range(2):
            home = 2 * p + j
            every = dot(xb[home // 3, 128 * (home % 3) : 128 * (home % 3 + 1), :], onehot)
            for g in range(4):
                kept = jnp.where(groups == 4 * j + g, every[FS * g : FS * (g + 1)], kept)
        wide[p // 8, z, x, mine, 128 * (p % 8) : 128 * (p % 8 + 1)] = kept.astype(BF16)

    def along_x(j):
        return (z * 4 + lax.rem(x + j, 4)) * 2 + core

    def along_z(j):
        return (lax.rem(z + j, 4) * 4 + x) * 2 + core

    def ag_copy(slot, part, device):
        return pltpu.make_async_remote_copy(
            src_ref=part,
            dst_ref=part,
            send_sem=ag_ss.at[slot],
            recv_sem=ag_rs.at[slot],
            device_id={"lists": device},
            device_id_type=MESH,
        )

    def phase(number):
        copies = []
        for half in range(2):
            near_one, far_one = (along_x, along_z) if half == 0 else (along_z, along_x)
            for j in range(1, 4):
                slot = 6 * (number - 1) + 3 * half + j - 1
                if number == 1:
                    copies.append((slot, wide.at[half, z, x, mine, :], near_one(j)))
                elif number == 2 and half == 0:
                    copies.append((slot, wide.at[half, z, :, mine, :], far_one(j)))
                elif number == 2:
                    copies.append((slot, wide.at[half, :, x, mine, :], far_one(j)))
            if number == 3:
                copies.append((12 + half, wide.at[half, :, :, mine, :], me + 1 - 2 * core))
        return copies

    def pieces(number, slot, part):
        if number == 1:
            return [part]
        if number == 2:
            return [part.at[q] for q in range(4)]
        return [part.at[q] for q in range(4)]

    def start_phase(number):
        for slot, part, device in phase(number):
            for piece in pieces(number, slot, part):
                ag_copy(slot, piece, device).start()

    def wait_phase(number):
        before = lambda v, j: lax.rem(v + 4 - j, 4)
        theirs = pl.ds(pl.multiple_of((1 - core) * FS, FS), FS)
        for half in range(2):
            for j in range(1, 4):
                slot = 6 * (number - 1) + 3 * half + j - 1
                if number == 1:
                    part = wide.at[half, z, before(x, j), mine, :] if half == 0 else wide.at[half, before(z, j), x, mine, :]
                elif number == 2:
                    part = wide.at[half, before(z, j), :, mine, :] if half == 0 else wide.at[half, :, before(x, j), mine, :]
                else:
                    slot, part = 12 + half, wide.at[half, :, :, theirs, :]
                if number < 3 or j == 1:
                    ag_copy(slot, part, peer(1)).wait_recv()

    start_phase(1)

    def across(i):
        chip = lax.rem(z + lax.rem(i, 4), 4) * 4 + lax.rem(x + lax.rem(lax.div(i, 4) + i, 4), 4)
        return [chip * 2 + core, chip * 2 + 1 - core]

    def vec_copy(part, k, owner, slice_of):
        low, high = PARTS[part]
        return pltpu.make_async_remote_copy(
            src_ref=send.at[k, low:high],
            dst_ref=recv.at[low:high, pl.ds(pl.multiple_of(slice_of * FS, FS), FS), :],
            send_sem=vec_ss.at[part],
            recv_sem=vec_rs.at[part],
            device_id={"lists": owner},
            device_id_type=MESH,
        )

    def own_copy(part):
        low, high = PARTS[part]
        return pltpu.make_async_copy(
            send.at[0, low:high],
            recv.at[low:high, pl.ds(pl.multiple_of(me * FS, FS), FS), :],
            own_sem.at[part],
        )

    def send_to(part, i):
        owners = across(i)

        @pl.when(i == 0)
        def _():
            own_copy(part).start()

        @pl.when(i > 0)
        def _():
            vec_copy(part, 2 * i, owners[0], me).start()

        vec_copy(part, 2 * i + 1, owners[1], me).start()

    def select_part(part):
        @pl.loop(0, N // GROUP)
        def _(i):
            chips = [GROUP // 2 * i + j for j in range(GROUP // 2)]
            owners = [owner for chip in chips for owner in across(chip)]
            for b in range(*PARTS[part]):
                entries = jnp.concatenate([at_owner(b, owner) for owner in owners], axis=1)
                every = dot(xb[b], onehots(iota((256, 128 * GROUP), 0) == (entries & 255)))
                groups = jnp.broadcast_to((entries >> 8) & 63, (FS, 128 * GROUP))
                kept = jnp.zeros((FS, 128 * GROUP), F32)
                for g in range(12):
                    kept = jnp.where(groups == g, every[FS * g : FS * (g + 1)], kept)
                kept = kept.astype(BF16)
                for j in range(GROUP):
                    send[GROUP * i + j, b] = kept[:, 128 * j : 128 * (j + 1)]

            if part == 0:
                for chip in chips:
                    send_to(part, chip)

                @pl.when(i == EARLY)
                def _():
                    wait_phase(1)
                    start_phase(2)

    for part in range(len(PARTS)):
        select_part(part)

    @pl.loop(0, NEARS)
    def _(t):
        lanes = pl.ds(pl.multiple_of(t * NEAR, 128), NEAR)
        onehot = onehots(iota((LISTS, NEAR), 0) == local_ref[:, lanes])
        near[:, lanes] = dot(cent_t[...], onehot).astype(BF16)

        for part, tile in LATER.items():

            @pl.when(t == tile)
            def _():
                @pl.loop(0, N // 2)
                def _(i):
                    send_to(part, i)

        @pl.when(t == PHASE)
        def _():
            wait_phase(2)
            start_phase(3)

    def encode(width, lanes):
        @pl.loop(0, 1)
        def _(i):
            rows = pl.ds(pl.multiple_of(i * 1024, 1024), 1024)
            turned = dot(rot_t[rows, :], resid[:, :width]).astype(BF16)
            for j in range(16):
                piece = turned[SUB * j : SUB * (j + 1)]
                sub[j, :SUB, :width] = piece
                squares = piece.astype(F32)
                length = jnp.sum(squares * squares, axis=0, keepdims=True)
                least = jnp.min(dot(codes[16 * i + j], sub[j, :, :width]), axis=0, keepdims=True)
                errs[pl.ds(16 * i + j, 1), lanes] = (length + least) * (1.0 / SUB)

    def minus(a, b):
        return (a.astype(F32) - b.astype(F32)).astype(BF16)

    def ret_copy(home, owner):
        return pltpu.make_async_remote_copy(
            src_ref=ret_send.at[home],
            dst_ref=ret_recv.at[owner],
            send_sem=ret_ss,
            recv_sem=ret_rs,
            device_id={"lists": home},
            device_id_type=MESH,
        )

    def overflow():
        wait_phase(3)

        @pl.loop(0, 2)
        def _(half):
            lanes = pl.ds(pl.multiple_of(half * 1024, 1024), 1024)

            @pl.loop(0, 4)
            def _(i):
                for j in range(4):
                    rows = pl.ds(pl.multiple_of(i * 256 + j * 64, 64), 64)
                    resid[rows, :] = minus(wide[half, i, j], near[rows, lanes])

            encode(1024, lanes)

    main_lanes = iota((BOOKS, 128), 1) < 64
    def main(part):
        low, high = PARTS[part]
        own_copy(part).wait()

        all_vectors(part).wait_recv()

        width, base = 128 * (high - low), FIRST + 128 * low

        @pl.loop(0, 4)
        def _(i):
            rows = pl.ds(pl.multiple_of(i * 256, 256), 256)
            for b in range(low, high):
                resid[rows, 128 * (b - low) : 128 * (b - low + 1)] = minus(
                    recv[b, rows, :], near[rows, FIRST + 128 * b : FIRST + 128 * (b + 1)]
                )

        encode(width, slice(base, base + width))

    def give_back(part):
        low, high = PARTS[part]
        for home in range(3 * low, min(3 * high, N)):
            least = errs[:, FIRST + 128 * (home // 3) : FIRST + 128 * (home // 3 + 1)]
            if home % 3:
                least = pltpu.roll(least, 128 - CAP * (home % 3), 1)
            more = errs[:, 128 * (home // 2) : 128 * (home // 2 + 1)]
            if home % 2 == 0:
                more = pltpu.roll(more, OVER, 1)
            ret_send[home] = jnp.where(main_lanes, least, more)

        @pl.loop(3 * low, min(3 * high, N))
        def _(home):
            @pl.when(home == me)
            def _():
                ret_recv[home] = ret_send[home]

            @pl.when(home != me)
            def _():
                ret_copy(home, me).start()

    overflow()
    for part in range(len(PARTS)):
        main(part)
        give_back(part)

    for j in range(1, DP):
        flag_copy(j, lax.rem(replica + DP - j, DP)).wait_recv()
        late = jnp.maximum(late, flag_all[lax.rem(replica + DP - j, DP)][:1, :1])
    flag_ref[...] = jnp.broadcast_to(late, (8, 128))

    all_tables().wait_send()
    for part in range(len(PARTS)):
        all_vectors(part).wait_send()
    for number in range(1, 4):
        for copy in phase(number):
            ag_copy(*copy).wait_send()
    for j in range(1, DP):
        flag_copy(j, replica).wait_send()

    for t in range(N // 2):
        arrive[t] = onehots(iota((256, HOME), 0) + 256 * t == code_ref[...])

    all_returns().wait_recv()

    total = jnp.zeros((2 * BOOKS, HOME), F32)
    for t in range(N // 2):
        got = jnp.concatenate([ret_recv[2 * t], ret_recv[2 * t + 1]], axis=1)
        high = got.astype(BF16)
        low = (got - high.astype(F32)).astype(BF16)
        total = total + dot(jnp.concatenate([high, low], axis=0), arrive[t])
    out_ref[...] = total[:BOOKS] + total[BOOKS:]

    all_returns().wait_send()


def fast(embeddings, assign, list_slot, centroids, rotation, codebook):
    vmem = pl.BlockSpec(memory_space=pltpu.VMEM)
    hbm = pl.BlockSpec(memory_space=pl.ANY)
    dma = pltpu.SemaphoreType.DMA
    return pl.pallas_call(
        kernel,
        out_shape=(jax.ShapeDtypeStruct((BOOKS, HOME), F32), jax.ShapeDtypeStruct((8, 128), I32)),
        in_specs=[hbm, vmem, vmem, hbm, hbm, vmem],
        out_specs=(vmem, vmem),
        scratch_shapes=[
            pltpu.VMEM((BLOCKS, 384, 256), BF16),
            pltpu.VMEM((N, BLOCKS, FS, 128), BF16),
            pltpu.VMEM((BLOCKS, D, 128), BF16),
            pltpu.VMEM((2, 4, 4, 2 * FS, 1024), BF16),
            pltpu.VMEM((D, NEARS * NEAR), BF16),
            pltpu.VMEM((LISTS, D), BF16),
            pltpu.VMEM((D, LISTS), BF16),
            pltpu.VMEM((D, D), BF16),
            pltpu.VMEM((D, D), BF16),
            pltpu.VMEM((BOOKS, CODES, 2 * SUB), BF16),
            pltpu.VMEM((16, 128), I32),
            pltpu.VMEM((N + 1, 16, 128), I32),
            pltpu.VMEM((BLOCKS, 3, 16, 128), I32),
            pltpu.VMEM((N // 2, 128), I32),
            pltpu.VMEM((1, NEARS * NEAR), I32),
            pltpu.VMEM((D, 1024), BF16),
            pltpu.VMEM((16, 2 * SUB, 1024), BF16),
            pltpu.VMEM((BOOKS, SLOTS), F32),
            pltpu.VMEM((1, HOME), I32),
            pltpu.VMEM((N, BOOKS, 128), F32),
            pltpu.VMEM((N, BOOKS, 128), F32),
            pltpu.VMEM((N // 2, 256, HOME), BF16),
            pltpu.VMEM((8, 128), I32),
            pltpu.VMEM((DP, 8, 128), I32),
            dma((2,)), dma, dma, dma((len(PARTS),)),
            dma, dma,
            dma((len(PARTS),)), dma((len(PARTS),)),
            dma, dma,
            dma((14,)), dma((14,)),
            dma((DP,)), dma((DP,)),
        ],
        compiler_params=pltpu.CompilerParams(
            collective_id=0, has_side_effects=True, vmem_limit_bytes=58 * 2**20
        ),
        name="encode",
    )(
        embeddings.T,
        assign.reshape(1, HOME),
        list_slot.reshape(512, 128),
        centroids,
        rotation.reshape(D, D),
        codebook.transpose(0, 2, 1),
    )


def route_rows(assigned, list_slot, list_width, owner_count):
    slot_index = jnp.take(list_slot, assigned)
    target = slot_index // list_width
    local_row = slot_index - target * list_width
    onehot = (target[..., None] == jnp.arange(owner_count, dtype=jnp.int32)).astype(jnp.int32)
    position = jnp.sum(jnp.cumsum(onehot, axis=-2) * onehot, axis=-1) - 1
    return (target, local_row, position)


def encode_rows(received, row_ids, centroids, rotation, codebook, code_norms):
    senders, slot_count, model_width = received.shape
    flattened = received.reshape(senders * slot_count, model_width)
    centre_rows = jnp.take(centroids, row_ids.reshape(-1), axis=0)
    residual = (flattened.astype(jnp.float32) - centre_rows.astype(jnp.float32)).astype(
        jnp.bfloat16
    )
    rotated = jnp.dot(residual, rotation[0], preferred_element_type=jnp.float32).astype(
        jnp.bfloat16
    )
    book_count, centres, sub_width = codebook.shape

    def one_book(book_index):
        subspace = lax.dynamic_slice_in_dim(rotated, book_index * sub_width, sub_width, 1)
        codewords = lax.dynamic_index_in_dim(codebook, book_index, 0, keepdims=False)
        norm_row = lax.dynamic_index_in_dim(code_norms, book_index, 0, keepdims=False)
        products = lax.dot_general(
            subspace, codewords, (((1,), (1,)), ((), ())), preferred_element_type=jnp.float32
        )
        lengths = jnp.sum(jnp.square(subspace.astype(jnp.float32)), axis=1)
        distance = lengths[:, None] + norm_row[None, :] - 2.0 * products
        return jnp.min(distance, axis=1) / sub_width

    errors = lax.map(one_book, jnp.arange(book_count, dtype=jnp.int32))
    errors = errors.reshape(book_count, senders, slot_count).transpose(1, 0, 2)
    return lax.all_to_all(errors, "lists", split_axis=0, concat_axis=0, tiled=True)


def general(embeddings, assign, list_slot, centroids, rotation, codebook):
    owner_count = lax.axis_size("lists")
    list_width = centroids.shape[0]
    home_rows = assign.shape[0]
    capacity = 3 * home_rows // owner_count
    model_width = rotation.shape[1]
    code_norms = jnp.sum(jnp.square(codebook.astype(jnp.float32)), axis=2)
    target, local_row, position = route_rows(assign, list_slot, list_width, owner_count)
    vectors = lax.all_to_all(embeddings, "lists", split_axis=0, concat_axis=1, tiled=True)
    outgoing = (
        jnp.zeros((owner_count, capacity, model_width), jnp.bfloat16)
        .at[target, position]
        .set(vectors)
    )
    row_ids = jnp.zeros((owner_count, capacity), jnp.int32).at[target, position].set(local_row)
    returned = encode_rows(
        lax.all_to_all(outgoing, "lists", split_axis=0, concat_axis=0, tiled=True),
        lax.all_to_all(row_ids, "lists", split_axis=0, concat_axis=0, tiled=True),
        centroids,
        rotation,
        codebook,
        code_norms,
    )
    return jnp.transpose(returned, (1, 0, 2))[:, target, position]


def shards(*arrays):
    errors, flag = fast(*arrays)
    return lax.cond(flag[0, 0] > 0, lambda: general(*arrays), lambda: errors)


def solution(mesh):
    placed = (
        P("dp", "lists"),
        P(("dp", "lists")),
        P(),
        P("lists", None),
        P("lists", None, None),
        P(),
    )
    return jax.shard_map(
        shards, mesh=mesh, in_specs=placed, out_specs=P(None, ("dp", "lists")), check_vma=False
    )
```

```python
import jax
import jax.numpy as jnp
from jax import lax
from jax.experimental import pallas as pl
from jax.experimental.pallas import tpu as pltpu
from jax.sharding import PartitionSpec as P

MESH = pl.DeviceIdType.MESH
F32 = jnp.float32
BF16 = jnp.bfloat16
I32 = jnp.int32

N = 32
DP = 4
HOME = 1024
D = 1024
FS = 32
LISTS = 2048
BOOKS, CODES, SUB = 16, 256, 64
CAP = 42
OVER = 64
BLOCKS = 11
PARTS = ((0, 4), (4, 8), (8, 11))
FIRST = N * OVER
SLOTS = FIRST + 128 * BLOCKS
NEAR = 512
GROUP = 8
EARLY = 1
PHASE = 2
LATER = {1: 1, 2: 3}
NEARS = -(-SLOTS // NEAR)
NOBODY = 32 << 8


def dot(a, b):
    return jnp.dot(a, b, preferred_element_type=F32)


def iota(shape, dim):
    return lax.broadcasted_iota(I32, shape, dim)


def onehots(mask):
    return mask.astype(F32).astype(BF16)


def routes(assign_ref, slots_ref):
    assigned = assign_ref[...]
    table = slots_ref[...].astype(F32).T.astype(I32)
    table = jnp.concatenate([table >> 8, table & 255], axis=0).astype(F32).astype(BF16)
    picked = dot(table, onehots(iota((512, HOME), 0) == (assigned >> 7)))
    low = iota((128, HOME), 0) == (assigned & 127)
    upper = jnp.sum(jnp.where(low, picked[:128], 0.0), axis=0, keepdims=True)
    lower = jnp.sum(jnp.where(low, picked[128:], 0.0), axis=0, keepdims=True)
    slot = upper.astype(I32) * 256 + lower.astype(I32)
    target, local = slot >> 11, slot & (LISTS - 1)
    mine = iota((N, HOME), 0) == target
    before = onehots(iota((HOME, HOME), 0) < iota((HOME, HOME), 1))
    ahead = dot(onehots(mine), before)
    rank = jnp.sum(jnp.where(mine, ahead, 0.0), axis=0, keepdims=True).astype(I32)
    over = rank >= CAP
    over_rank = dot(jnp.broadcast_to(onehots(over), (8, HOME)), before)[:1].astype(I32)
    segment = (target >= 11).astype(I32) + (target >= 22).astype(I32)
    row = jnp.where(over, 11, target - 11 * segment)
    lane = jnp.where(over, over_rank, CAP * segment + rank)
    mine = iota((16, HOME), 0) == row
    place = onehots(iota((128, HOME), 0) == lane)
    vector = iota((1, HOME), 1)
    fields = [vector & 255, vector >> 8, local & 255, local >> 8, jnp.ones_like(vector)]
    planes = [jnp.where(mine, field.astype(F32), 0.0) for field in fields]
    planes = jnp.concatenate(planes, axis=0).astype(BF16)
    held = lax.dot_general(planes, place, (((1,), (1,)), ((), ())), preferred_element_type=F32).astype(I32)
    index, group, local_low, local_high, valid = (held[16 * j : 16 * (j + 1)] for j in range(5))
    entry = index + (group << 8) + (local_low << 14) + (local_high << 22)
    entry = jnp.where(valid > 0, entry, NOBODY)
    return target * 128 + jnp.where(over, 64 + over_rank, rank), entry


def kernel(
    emb_ref, assign_ref, slots_ref, cent_ref, rot_ref, book_ref, out_ref, flag_ref,
    xb, send, recv, wide, near, cent, cent_t, rot, rot_t, codes, tab_own, tab_all, tab, tab_over, local_ref,
    resid, sub, errs, code_ref, ret_send, ret_recv, arrive, flag_own, flag_all,
    x_sem, c_sem, r_sem, own_sem, tab_ss, tab_rs, vec_ss, vec_rs, ret_ss, ret_rs, ag_ss, ag_rs, flag_ss, flag_rs,
):
    me = lax.axis_index("lists")
    replica = lax.axis_index("dp")
    core = lax.rem(me, 2)
    x = lax.rem(lax.div(me, 2), 4)
    z = lax.div(me, 8)

    def peer(k):
        return lax.rem(me + k, N)

    def all_of(ref, send_sem, recv_sem):
        return pltpu.make_async_remote_copy(
            src_ref=ref, dst_ref=ref, send_sem=send_sem, recv_sem=recv_sem,
            device_id={"lists": peer(1)}, device_id_type=MESH,
        )

    def all_tables():
        return all_of(tab_all.at[: N - 1], tab_ss, tab_rs)

    def all_vectors(part):
        low, high = PARTS[part]
        return all_of(send.at[1:, low:high], vec_ss.at[part], vec_rs.at[part])

    def all_returns():
        return all_of(ret_recv.at[: N - 1], ret_ss, ret_rs)

    barrier = pltpu.get_barrier_semaphore()

    @pl.loop(1, N)
    def _(k):
        pl.semaphore_signal(barrier, inc=1, device_id={"lists": peer(k)}, device_id_type=MESH)

    for j in range(1, DP):
        other = lax.rem(replica + j, DP)
        pl.semaphore_signal(barrier, inc=1, device_id={"dp": other}, device_id_type=MESH)

    def x_copy(t):
        block = lax.div(t, 12)
        group = t - block * 12
        return pltpu.make_async_copy(
            emb_ref.at[:, pl.ds(pl.multiple_of(t * 256, 256), 256)],
            xb.at[block, pl.ds(pl.multiple_of(group * FS, FS), FS), :],
            x_sem.at[lax.div(t, 120)],
        )

    c_copy = pltpu.make_async_copy(cent_ref, cent, c_sem)
    r_copy = pltpu.make_async_copy(rot_ref, rot, r_sem)
    c_copy.start()
    r_copy.start()

    code, entry = routes(assign_ref, slots_ref)
    code_ref[...] = code
    tab_own[...] = entry

    pl.semaphore_wait(barrier, N - 1 + DP - 1)

    def tab_copy(k, home):
        return pltpu.make_async_remote_copy(
            src_ref=tab_own,
            dst_ref=tab_all.at[home],
            send_sem=tab_ss,
            recv_sem=tab_rs,
            device_id={"lists": peer(k)},
            device_id_type=MESH,
        )

    @pl.loop(1, N)
    def _(k):
        tab_copy(k, me).start()

    @pl.loop(0, 128)
    def _(t):
        x_copy(t).start()

    tab_all[me] = entry
    tab_all[N] = jnp.full((16, 128), NOBODY, I32)
    xb[BLOCKS - 1, 256:, :] = jnp.zeros((128, 256), BF16)
    sub[:, SUB:, :] = jnp.ones((16, SUB, 1024), BF16)

    @pl.loop(0, BOOKS)
    def _(m):
        words = book_ref[m].astype(F32)
        norm = jnp.sum(words * words, axis=0, keepdims=True)
        first = norm.astype(BF16).astype(F32)
        second = (norm - first).astype(BF16).astype(F32)
        third = norm - first - second
        row = iota((SUB, CODES), 0)
        extra = jnp.where(row == 0, first, jnp.where(row == 1, second, jnp.where(row == 2, third, 0.0)))
        codes[m] = jnp.concatenate([words * -2.0, extra], axis=0).T.astype(BF16)

    r_copy.wait()
    c_copy.wait()

    @pl.loop(0, 4)
    def _(i):
        rows = pl.multiple_of(i * 256, 256)
        for j in range(4):
            rot_t[256 * j : 256 * (j + 1), pl.ds(rows, 256)] = rot[pl.ds(rows, 256), 256 * j : 256 * (j + 1)].T

    @pl.loop(0, 8)
    def _(i):
        rows = pl.multiple_of(i * 256, 256)
        for j in range(4):
            cent_t[256 * j : 256 * (j + 1), pl.ds(rows, 256)] = cent[pl.ds(rows, 256), 256 * j : 256 * (j + 1)].T

    pltpu.make_async_copy(xb.at[:10], xb.at[:10], x_sem.at[0]).wait()
    pltpu.make_async_copy(xb.at[10, :256], xb.at[10, :256], x_sem.at[1]).wait()

    all_tables().wait_recv()

    lane = iota((16, 128), 1)

    @pl.loop(0, BLOCKS)
    def _(b):
        homes = [tab_all[3 * b + j] + (j << 10) for j in range(3)]
        for s in range(3):
            moved = [pltpu.roll(homes[j], (CAP * (j - s)) % 128, 1) if j != s else homes[j] for j in range(3)]
            found = jnp.where(lane < CAP, moved[0], jnp.where(lane < 2 * CAP, moved[1], moved[2]))
            tab[b, s] = jnp.where(lane < 3 * CAP, found, NOBODY)

    late = jnp.zeros((1, 128), I32)
    first_half = iota((1, 128), 1) < OVER
    for p in range(N // 2):
        left, right = tab_all[2 * p, 11:12, :], tab_all[2 * p + 1, 11:12, :]
        tab_over[p : p + 1, :] = jnp.where(first_half, left, pltpu.roll(right, OVER, 1) + (4 << 8))
        for row in (left, right):
            late = jnp.where(first_half | (((row >> 8) & 63) >= 32), late, 1)
        local_ref[:, 128 * p : 128 * (p + 1)] = tab_over[p : p + 1, :] >> 14
    late = jnp.max(late, axis=1, keepdims=True)
    flag_own[...] = jnp.broadcast_to(late, (8, 128))

    def flag_copy(j, origin):
        return pltpu.make_async_remote_copy(
            src_ref=flag_own,
            dst_ref=flag_all.at[origin],
            send_sem=flag_ss.at[j],
            recv_sem=flag_rs.at[j],
            device_id={"dp": lax.rem(replica + j, DP)},
            device_id_type=MESH,
        )

    for j in range(1, DP):
        flag_copy(j, replica).start()

    def at_owner(b, owner):
        segment = lax.div(owner, 11)
        return tab[b, segment, pl.ds(owner - 11 * segment, 1), :]

    local_ref[:, SLOTS:] = jnp.zeros((1, NEARS * NEAR - SLOTS), I32)
    for b in range(BLOCKS):
        local_ref[:, FIRST + 128 * b : FIRST + 128 * (b + 1)] = at_owner(b, me) >> 14

    mine = pl.ds(pl.multiple_of(core * FS, FS), FS)
    for p in range(N // 2):
        entries = tab_over[p : p + 1, :]
        onehot = onehots(iota((256, 128), 0) == (entries & 255))
        groups = jnp.broadcast_to((entries >> 8) & 63, (FS, 128))
        kept = jnp.zeros((FS, 128), F32)
        for j in range(2):
            home = 2 * p + j
            every = dot(xb[home // 3, 128 * (home % 3) : 128 * (home % 3 + 1), :], onehot)
            for g in range(4):
                kept = jnp.where(groups == 4 * j + g, every[FS * g : FS * (g + 1)], kept)
        wide[p // 8, z, x, mine, 128 * (p % 8) : 128 * (p % 8 + 1)] = kept.astype(BF16)

    def along_x(j):
        return (z * 4 + lax.rem(x + j, 4)) * 2 + core

    def along_z(j):
        return (lax.rem(z + j, 4) * 4 + x) * 2 + core

    def ag_copy(slot, part, device):
        return pltpu.make_async_remote_copy(
            src_ref=part,
            dst_ref=part,
            send_sem=ag_ss.at[slot],
            recv_sem=ag_rs.at[slot],
            device_id={"lists": device},
            device_id_type=MESH,
        )

    def phase(number):
        copies = []
        for half in range(2):
            near_one, far_one = (along_x, along_z) if half == 0 else (along_z, along_x)
            for j in range(1, 4):
                slot = 6 * (number - 1) + 3 * half + j - 1
                if number == 1:
                    copies.append((slot, wide.at[half, z, x, mine, :], near_one(j)))
                elif number == 2 and half == 0:
                    copies.append((slot, wide.at[half, z, :, mine, :], far_one(j)))
                elif number == 2:
                    copies.append((slot, wide.at[half, :, x, mine, :], far_one(j)))
            if number == 3:
                copies.append((12 + half, wide.at[half, :, :, mine, :], me + 1 - 2 * core))
        return copies

    def pieces(number, slot, part):
        if number == 1:
            return [part]
        if number == 2:
            return [part.at[q] for q in range(4)]
        return [part.at[q] for q in range(4)]

    def start_phase(number):
        for slot, part, device in phase(number):
            for piece in pieces(number, slot, part):
                ag_copy(slot, piece, device).start()

    def wait_phase(number):
        before = lambda v, j: lax.rem(v + 4 - j, 4)
        theirs = pl.ds(pl.multiple_of((1 - core) * FS, FS), FS)
        for half in range(2):
            for j in range(1, 4):
                slot = 6 * (number - 1) + 3 * half + j - 1
                if number == 1:
                    part = wide.at[half, z, before(x, j), mine, :] if half == 0 else wide.at[half, before(z, j), x, mine, :]
                elif number == 2:
                    part = wide.at[half, before(z, j), :, mine, :] if half == 0 else wide.at[half, :, before(x, j), mine, :]
                else:
                    slot, part = 12 + half, wide.at[half, :, :, theirs, :]
                if number < 3 or j == 1:
                    ag_copy(slot, part, peer(1)).wait_recv()

    start_phase(1)

    def across(i):
        chip = lax.rem(z + lax.rem(i, 4), 4) * 4 + lax.rem(x + lax.rem(lax.div(i, 4) + i, 4), 4)
        return [chip * 2 + core, chip * 2 + 1 - core]

    def vec_copy(part, k, owner, slice_of):
        low, high = PARTS[part]
        return pltpu.make_async_remote_copy(
            src_ref=send.at[k, low:high],
            dst_ref=recv.at[low:high, pl.ds(pl.multiple_of(slice_of * FS, FS), FS), :],
            send_sem=vec_ss.at[part],
            recv_sem=vec_rs.at[part],
            device_id={"lists": owner},
            device_id_type=MESH,
        )

    def own_copy(part):
        low, high = PARTS[part]
        return pltpu.make_async_copy(
            send.at[0, low:high],
            recv.at[low:high, pl.ds(pl.multiple_of(me * FS, FS), FS), :],
            own_sem.at[part],
        )

    def send_to(part, i):
        owners = across(i)

        @pl.when(i == 0)
        def _():
            own_copy(part).start()

        @pl.when(i > 0)
        def _():
            vec_copy(part, 2 * i, owners[0], me).start()

        vec_copy(part, 2 * i + 1, owners[1], me).start()

    def select_part(part):
        @pl.loop(0, N // GROUP)
        def _(i):
            chips = [GROUP // 2 * i + j for j in range(GROUP // 2)]
            owners = [owner for chip in chips for owner in across(chip)]
            for b in range(*PARTS[part]):
                entries = jnp.concatenate([at_owner(b, owner) for owner in owners], axis=1)
                every = dot(xb[b], onehots(iota((256, 128 * GROUP), 0) == (entries & 255)))
                groups = jnp.broadcast_to((entries >> 8) & 63, (FS, 128 * GROUP))
                kept = jnp.zeros((FS, 128 * GROUP), F32)
                for g in range(12):
                    kept = jnp.where(groups == g, every[FS * g : FS * (g + 1)], kept)
                kept = kept.astype(BF16)
                for j in range(GROUP):
                    send[GROUP * i + j, b] = kept[:, 128 * j : 128 * (j + 1)]

            if part == 0:
                for chip in chips:
                    send_to(part, chip)

                @pl.when(i == EARLY)
                def _():
                    wait_phase(1)
                    start_phase(2)

    for part in range(len(PARTS)):
        select_part(part)

    @pl.loop(0, NEARS)
    def _(t):
        lanes = pl.ds(pl.multiple_of(t * NEAR, 128), NEAR)
        onehot = onehots(iota((LISTS, NEAR), 0) == local_ref[:, lanes])
        near[:, lanes] = dot(cent_t[...], onehot).astype(BF16)

        for part, tile in LATER.items():

            @pl.when(t == tile)
            def _():
                @pl.loop(0, N // 2)
                def _(i):
                    send_to(part, i)

        @pl.when(t == PHASE)
        def _():
            wait_phase(2)
            start_phase(3)

    def encode(width, lanes):
        @pl.loop(0, 1)
        def _(i):
            rows = pl.ds(pl.multiple_of(i * 1024, 1024), 1024)
            turned = dot(rot_t[rows, :], resid[:, :width]).astype(BF16)
            for j in range(16):
                piece = turned[SUB * j : SUB * (j + 1)]
                sub[j, :SUB, :width] = piece
                squares = piece.astype(F32)
                length = jnp.sum(squares * squares, axis=0, keepdims=True)
                least = jnp.min(dot(codes[16 * i + j], sub[j, :, :width]), axis=0, keepdims=True)
                errs[pl.ds(16 * i + j, 1), lanes] = (length + least) * (1.0 / SUB)

    def minus(a, b):
        return (a.astype(F32) - b.astype(F32)).astype(BF16)

    def ret_copy(home, owner):
        return pltpu.make_async_remote_copy(
            src_ref=ret_send.at[home],
            dst_ref=ret_recv.at[owner],
            send_sem=ret_ss,
            recv_sem=ret_rs,
            device_id={"lists": home},
            device_id_type=MESH,
        )

    def overflow():
        wait_phase(3)

        @pl.loop(0, 2)
        def _(half):
            lanes = pl.ds(pl.multiple_of(half * 1024, 1024), 1024)

            @pl.loop(0, 4)
            def _(i):
                for j in range(4):
                    rows = pl.ds(pl.multiple_of(i * 256 + j * 64, 64), 64)
                    resid[rows, :] = minus(wide[half, i, j], near[rows, lanes])

            encode(1024, lanes)

    main_lanes = iota((BOOKS, 128), 1) < 64
    def main(parts):
        low, high = PARTS[parts[0]][0], PARTS[parts[-1]][1]
        for part in parts:
            own_copy(part).wait()
            all_vectors(part).wait_recv()


        width, base = 128 * (high - low), FIRST + 128 * low

        @pl.loop(0, 4)
        def _(i):
            rows = pl.ds(pl.multiple_of(i * 256, 256), 256)
            for b in range(low, high):
                resid[rows, 128 * (b - low) : 128 * (b - low + 1)] = minus(
                    recv[b, rows, :], near[rows, FIRST + 128 * b : FIRST + 128 * (b + 1)]
                )

        encode(width, slice(base, base + width))

    def give_back(part):
        low, high = PARTS[part]
        for home in range(3 * low, min(3 * high, N)):
            least = errs[:, FIRST + 128 * (home // 3) : FIRST + 128 * (home // 3 + 1)]
            if home % 3:
                least = pltpu.roll(least, 128 - CAP * (home % 3), 1)
            more = errs[:, 128 * (home // 2) : 128 * (home // 2 + 1)]
            if home % 2 == 0:
                more = pltpu.roll(more, OVER, 1)
            ret_send[home] = jnp.where(main_lanes, least, more)

        @pl.loop(3 * low, min(3 * high, N))
        def _(home):
            @pl.when(home == me)
            def _():
                ret_recv[home] = ret_send[home]

            @pl.when(home != me)
            def _():
                ret_copy(home, me).start()

    overflow()
    for parts in ((0, 1), (2,)):
        main(parts)
        for part in parts:
            give_back(part)

    for j in range(1, DP):
        flag_copy(j, lax.rem(replica + DP - j, DP)).wait_recv()
        late = jnp.maximum(late, flag_all[lax.rem(replica + DP - j, DP)][:1, :1])
    flag_ref[...] = jnp.broadcast_to(late, (8, 128))

    all_tables().wait_send()
    for part in range(len(PARTS)):
        all_vectors(part).wait_send()
    for number in range(1, 4):
        for copy in phase(number):
            ag_copy(*copy).wait_send()
    for j in range(1, DP):
        flag_copy(j, replica).wait_send()

    for t in range(N // 2):
        arrive[t] = onehots(iota((256, HOME), 0) + 256 * t == code_ref[...])

    all_returns().wait_recv()

    total = jnp.zeros((2 * BOOKS, HOME), F32)
    for t in range(N // 2):
        got = jnp.concatenate([ret_recv[2 * t], ret_recv[2 * t + 1]], axis=1)
        high = got.astype(BF16)
        low = (got - high.astype(F32)).astype(BF16)
        total = total + dot(jnp.concatenate([high, low], axis=0), arrive[t])
    out_ref[...] = total[:BOOKS] + total[BOOKS:]

    all_returns().wait_send()


def fast(embeddings, assign, list_slot, centroids, rotation, codebook):
    vmem = pl.BlockSpec(memory_space=pltpu.VMEM)
    hbm = pl.BlockSpec(memory_space=pl.ANY)
    dma = pltpu.SemaphoreType.DMA
    return pl.pallas_call(
        kernel,
        out_shape=(jax.ShapeDtypeStruct((BOOKS, HOME), F32), jax.ShapeDtypeStruct((8, 128), I32)),
        in_specs=[hbm, vmem, vmem, hbm, hbm, vmem],
        out_specs=(vmem, vmem),
        scratch_shapes=[
            pltpu.VMEM((BLOCKS, 384, 256), BF16),
            pltpu.VMEM((N, BLOCKS, FS, 128), BF16),
            pltpu.VMEM((BLOCKS, D, 128), BF16),
            pltpu.VMEM((2, 4, 4, 2 * FS, 1024), BF16),
            pltpu.VMEM((D, NEARS * NEAR), BF16),
            pltpu.VMEM((LISTS, D), BF16),
            pltpu.VMEM((D, LISTS), BF16),
            pltpu.VMEM((D, D), BF16),
            pltpu.VMEM((D, D), BF16),
            pltpu.VMEM((BOOKS, CODES, 2 * SUB), BF16),
            pltpu.VMEM((16, 128), I32),
            pltpu.VMEM((N + 1, 16, 128), I32),
            pltpu.VMEM((BLOCKS, 3, 16, 128), I32),
            pltpu.VMEM((N // 2, 128), I32),
            pltpu.VMEM((1, NEARS * NEAR), I32),
            pltpu.VMEM((D, 1024), BF16),
            pltpu.VMEM((16, 2 * SUB, 1024), BF16),
            pltpu.VMEM((BOOKS, SLOTS), F32),
            pltpu.VMEM((1, HOME), I32),
            pltpu.VMEM((N, BOOKS, 128), F32),
            pltpu.VMEM((N, BOOKS, 128), F32),
            pltpu.VMEM((N // 2, 256, HOME), BF16),
            pltpu.VMEM((8, 128), I32),
            pltpu.VMEM((DP, 8, 128), I32),
            dma((2,)), dma, dma, dma((len(PARTS),)),
            dma, dma,
            dma((len(PARTS),)), dma((len(PARTS),)),
            dma, dma,
            dma((14,)), dma((14,)),
            dma((DP,)), dma((DP,)),
        ],
        compiler_params=pltpu.CompilerParams(
            collective_id=0, has_side_effects=True, vmem_limit_bytes=58 * 2**20
        ),
        name="encode",
    )(
        embeddings.T,
        assign.reshape(1, HOME),
        list_slot.reshape(512, 128),
        centroids,
        rotation.reshape(D, D),
        codebook.transpose(0, 2, 1),
    )


def route_rows(assigned, list_slot, list_width, owner_count):
    slot_index = jnp.take(list_slot, assigned)
    target = slot_index // list_width
    local_row = slot_index - target * list_width
    onehot = (target[..., None] == jnp.arange(owner_count, dtype=jnp.int32)).astype(jnp.int32)
    position = jnp.sum(jnp.cumsum(onehot, axis=-2) * onehot, axis=-1) - 1
    return (target, local_row, position)


def encode_rows(received, row_ids, centroids, rotation, codebook, code_norms):
    senders, slot_count, model_width = received.shape
    flattened = received.reshape(senders * slot_count, model_width)
    centre_rows = jnp.take(centroids, row_ids.reshape(-1), axis=0)
    residual = (flattened.astype(jnp.float32) - centre_rows.astype(jnp.float32)).astype(
        jnp.bfloat16
    )
    rotated = jnp.dot(residual, rotation[0], preferred_element_type=jnp.float32).astype(
        jnp.bfloat16
    )
    book_count, centres, sub_width = codebook.shape

    def one_book(book_index):
        subspace = lax.dynamic_slice_in_dim(rotated, book_index * sub_width, sub_width, 1)
        codewords = lax.dynamic_index_in_dim(codebook, book_index, 0, keepdims=False)
        norm_row = lax.dynamic_index_in_dim(code_norms, book_index, 0, keepdims=False)
        products = lax.dot_general(
            subspace, codewords, (((1,), (1,)), ((), ())), preferred_element_type=jnp.float32
        )
        lengths = jnp.sum(jnp.square(subspace.astype(jnp.float32)), axis=1)
        distance = lengths[:, None] + norm_row[None, :] - 2.0 * products
        return jnp.min(distance, axis=1) / sub_width

    errors = lax.map(one_book, jnp.arange(book_count, dtype=jnp.int32))
    errors = errors.reshape(book_count, senders, slot_count).transpose(1, 0, 2)
    return lax.all_to_all(errors, "lists", split_axis=0, concat_axis=0, tiled=True)


def general(embeddings, assign, list_slot, centroids, rotation, codebook):
    owner_count = lax.axis_size("lists")
    list_width = centroids.shape[0]
    home_rows = assign.shape[0]
    capacity = 3 * home_rows // owner_count
    model_width = rotation.shape[1]
    code_norms = jnp.sum(jnp.square(codebook.astype(jnp.float32)), axis=2)
    target, local_row, position = route_rows(assign, list_slot, list_width, owner_count)
    vectors = lax.all_to_all(embeddings, "lists", split_axis=0, concat_axis=1, tiled=True)
    outgoing = (
        jnp.zeros((owner_count, capacity, model_width), jnp.bfloat16)
        .at[target, position]
        .set(vectors)
    )
    row_ids = jnp.zeros((owner_count, capacity), jnp.int32).at[target, position].set(local_row)
    returned = encode_rows(
        lax.all_to_all(outgoing, "lists", split_axis=0, concat_axis=0, tiled=True),
        lax.all_to_all(row_ids, "lists", split_axis=0, concat_axis=0, tiled=True),
        centroids,
        rotation,
        codebook,
        code_norms,
    )
    return jnp.transpose(returned, (1, 0, 2))[:, target, position]


def shards(*arrays):
    errors, flag = fast(*arrays)
    return lax.cond(flag[0, 0] > 0, lambda: general(*arrays), lambda: errors)


def solution(mesh):
    placed = (
        P("dp", "lists"),
        P(("dp", "lists")),
        P(),
        P("lists", None),
        P("lists", None, None),
        P(),
    )
    return jax.shard_map(
        shards, mesh=mesh, in_specs=placed, out_specs=P(None, ("dp", "lists")), check_vma=False
    )
```
